512 devices in a mesh: roll: 16 (over z), fsdp: 32 (over x, y, core).
Axes of the slice: x: 4, y: 4, z: 16, core: 2. Of those that a mesh axis runs over, the one named last changes fastest.
Arguments:
- hidden_rows: bfloat16 [256, 5120], P('roll', 'fsdp'), may hold values from -6 to 6
- embed_rows: bfloat16 [256, 5120], P('roll', 'fsdp'), may hold values from -6 to 6
- target_rows: bfloat16 [256, 5120], P('roll'), may hold values from -6 to 6
- counts: int32 [16], P('roll'), may hold values from 1 to 16, 128 in all
- fc_weight: bfloat16 [2, 5120, 5120], P(None, 'fsdp', 'roll'), may hold values from -0.0625 to 0.0625
- norm_gain: float32 [5120], P('roll'), may hold values from 0.35 to 15
- gate_weight: bfloat16 [5120, 25600], P('roll', 'fsdp'), may hold values from -0.078125 to 0.078125
- up_weight: bfloat16 [5120, 25600], P('roll', 'fsdp'), may hold values from -0.078125 to 0.078125
- down_weight: bfloat16 [25600, 5120], P('fsdp', 'roll'), may hold values from -0.0390625 to 0.0390625
Outputs:
- grad_fc: float32 [2, 5120, 5120], P(None, 'fsdp', 'roll')
- grad_gain: float32 [5120], P('roll')
- grad_gate: bfloat16 [5120, 25600], P('roll', 'fsdp')
- grad_up: bfloat16 [5120, 25600], P('roll', 'fsdp')
- grad_down: float32 [25600, 5120], P('fsdp', 'roll')
The draws below stay inside these ranges and needn't reach their ends.
Inputs may be any that keep to these rules, and one draw needn't show every extreme that they name: counts[e] of engine e's slots, its first ones, hold live rows; the counts sum to 128 and the largest equals 16.
All inputs are finite; a program needn't handle non-finite values. No bound on the sum of `counts` on one device may be relied on, other than what follows from the above.
Results may differ from the reference program's by a relative error of at most 0.012.
Values may be sent and summed in bfloat16 or wider, within the bound.
A program may use at most 64 MiB of HBM per device.

```python
import math
import jax
import jax.numpy as jnp
import numpy as np
from jax import lax

D = 5120
FF = 25600
CAP = 16
ROWS = 128
SLOTS = 256
N_ROLL = 16


def draw_norm_gain(key, part):
    key = jax.random.fold_in(key, 7)
    position = jnp.arange(D, dtype=jnp.float32) / (D - 1)
    ramp = jnp.exp(math.log(6.0) * position)
    rough = jax.random.uniform(key, (D,), jnp.float32, 0.7, 1.3)
    return (ramp * rough).astype(jnp.float32)


def block_scale(stream_key, dims, split, smallest, top_value):
    def one(axis_at, parts):
        heights = jax.random.uniform(jax.random.fold_in(jax.random.fold_in(stream_key, 6), axis_at), (parts,), jnp.float32, smallest / len(split), top_value / len(split))
        return jnp.repeat(jnp.exp(heights), dims[axis_at] // parts).reshape((-1,) + (1,) * (len(dims) - axis_at - 1))

    level = one(*split[0])
    for cut in split[1:]:
        level = level * one(*cut)
    return level


def length_profile(count, total, bound, lean):
    portions = [(1 << 20) // math.isqrt(standing ** lean) + 1 for standing in range(2, count + 1)]
    spare, holding = total - bound - (count - 1), [1] * (count - 1)
    while spare > 0:
        candidates = [i for i in range(count - 1) if holding[i] < bound]
        whole, remaining = sum([portions[i] for i in candidates]), spare
        for i in candidates:
            more = min(bound - holding[i], max(1, remaining * portions[i] // whole), spare)
            holding[i] = holding[i] + more
            spare = spare - more
    return np.array([bound] + holding)


def uneven(own_key, amount, total, reach, skew):
    if amount == 2:
        one = jax.random.randint(own_key, (), max(1, total - reach), min(reach, total - 1) + 1)
        return jnp.stack([one, total - one])
    lengths = jnp.asarray(length_profile(amount, total, reach, skew), jnp.int32)
    twos = (amount - 1) // 2
    donor, sink = lengths[1:1 + 2 * twos:2], lengths[2:2 + 2 * twos:2]
    margin = jnp.minimum(donor - 1, reach - sink)
    passed = jax.random.randint(jax.random.fold_in(own_key, 1), (twos,), 0, 1 << 20) % (margin + 1)
    lengths = lengths.at[1:1 + 2 * twos:2].set(donor - passed).at[2:2 + 2 * twos:2].set(sink + passed)
    return lengths[jax.random.permutation(jax.random.fold_in(own_key, 2), amount)]


def bell_draw(key, extent, deviation, most, split=(), kind=jnp.bfloat16):
    array = deviation * jax.random.normal(key, extent, jnp.float32)
    if split:
        array = array * block_scale(key, extent, split, -0.22, 0.18)
    return jnp.clip(array, -most, most).astype(kind)


def setup_inputs(seed: int = 0) -> dict:
    keys = jax.random.split(jax.random.key(seed), 10)
    return {
        "hidden_rows": bell_draw(keys[0], (SLOTS, D), 1.0, 6.0, ((0, 16), (1, 32))),
        "embed_rows": bell_draw(keys[1], (SLOTS, D), 1.0, 6.0, ((0, 16), (1, 32))),
        "target_rows": bell_draw(keys[2], (SLOTS, D), 1.0, 6.0, ((0, 16),)),
        "counts": uneven(keys[3], N_ROLL, ROWS, CAP, 2).astype(jnp.int32),
        "fc_weight": bell_draw(keys[4], (2, D, D), (2 * D) ** -0.5, 0.0625, ((1, 32), (2, 16))),
        "norm_gain": draw_norm_gain(jax.random.fold_in(keys[9], 71), 0),
        "gate_weight": bell_draw(keys[6], (D, FF), D ** -0.5, 0.078125, ((0, 16), (1, 32))),
        "up_weight": bell_draw(keys[7], (D, FF), D ** -0.5, 0.078125, ((0, 16), (1, 32))),
        "down_weight": bell_draw(keys[8], (FF, D), FF ** -0.5, 0.0390625, ((0, 32), (1, 16))),
    }


epsilon = 1e-06

def source_slots(counts, capacity, row_total):
    counts = counts.astype(jnp.int32)
    row_ends = jnp.cumsum(counts).astype(jnp.int32)
    row_starts = (row_ends - counts).astype(jnp.int32)
    positions = jnp.arange(row_total, dtype=jnp.int32)
    engine_ids = lax.optimization_barrier(jnp.sum((row_ends[None, :] <= positions[:, None]).astype(jnp.int32), axis=1)).astype(jnp.int32)
    matches = engine_ids[:, None] == jnp.arange(counts.shape[0], dtype=jnp.int32)[None, :]
    offsets = lax.optimization_barrier(jnp.sum(jnp.where(matches, row_starts[None, :], 0), axis=1)).astype(jnp.int32)
    return (engine_ids * capacity + positions - offsets).astype(jnp.int32)

def reference(hidden_rows, embed_rows, target_rows, counts, fc_weight, norm_gain, gate_weight, up_weight, down_weight):
    source_rows = source_slots(counts, CAP, ROWS)
    embeds = jnp.take(embed_rows, source_rows, axis=0)
    hiddens = jnp.take(hidden_rows, source_rows, axis=0)
    targets = jnp.take(target_rows, source_rows, axis=0).astype(jnp.float32)
    mixed_in = jnp.dot(embeds, fc_weight[0], preferred_element_type=jnp.float32) + jnp.dot(hiddens, fc_weight[1], preferred_element_type=jnp.float32)
    inverse_rms = lax.rsqrt(lax.optimization_barrier(jnp.sum(mixed_in * mixed_in, axis=1, keepdims=True)) / D + epsilon)
    normed = (mixed_in * inverse_rms * norm_gain).astype(jnp.bfloat16)
    gate_pre = jnp.dot(normed, gate_weight, preferred_element_type=jnp.float32)
    up_pre = jnp.dot(normed, up_weight, preferred_element_type=jnp.float32)
    activated = (jax.nn.silu(gate_pre) * up_pre).astype(jnp.bfloat16)
    drafted = mixed_in + jnp.dot(activated, down_weight, preferred_element_type=jnp.float32)
    loss_grad = (drafted - targets) * (1.0 / math.sqrt(ROWS))
    loss_grad_b = loss_grad.astype(jnp.bfloat16)
    grad_down = jnp.dot(activated.T, loss_grad_b, preferred_element_type=jnp.float32)
    back_act = jnp.dot(loss_grad_b, down_weight.T, preferred_element_type=jnp.float32)
    sigmoid_gate = jax.nn.sigmoid(gate_pre)
    back_gate = (back_act * up_pre * sigmoid_gate * (1.0 + gate_pre * (1.0 - sigmoid_gate))).astype(jnp.bfloat16)
    back_up = (back_act * gate_pre * sigmoid_gate).astype(jnp.bfloat16)
    grad_gate = jnp.dot(normed.T, back_gate, preferred_element_type=jnp.float32).astype(jnp.bfloat16)
    grad_up = jnp.dot(normed.T, back_up, preferred_element_type=jnp.float32).astype(jnp.bfloat16)
    back_norm = jnp.dot(back_gate, gate_weight.T, preferred_element_type=jnp.float32) + jnp.dot(back_up, up_weight.T, preferred_element_type=jnp.float32)
    grad_gain = lax.optimization_barrier(jnp.sum(back_norm * mixed_in * inverse_rms, axis=0))
    gained = back_norm * norm_gain
    inner = lax.optimization_barrier(jnp.sum(gained * mixed_in, axis=1, keepdims=True)) / D
    back_mix = loss_grad + inverse_rms * gained - mixed_in * inverse_rms ** 3 * inner
    back_mix_b = back_mix.astype(jnp.bfloat16)
    grad_fc = jnp.stack([jnp.dot(embeds.T, back_mix_b, preferred_element_type=jnp.float32), jnp.dot(hiddens.T, back_mix_b, preferred_element_type=jnp.float32)])
    return (grad_fc, grad_gain, grad_gate, grad_up, grad_down)
```

```python
import math

import jax
import jax.numpy as jnp
from jax import lax
from jax.experimental import pallas as pl
from jax.experimental.pallas import tpu as pltpu
from jax.sharding import PartitionSpec as P

D = 5120
ROWS = 128
CAP = 16
NZ = 16
NF = 32
DB = 320
DP = 384
FB = 800
FP = 896
PIECE = DB // NF
META = 832
EPS = 1e-06
SCALE = 1.0 / math.sqrt(ROWS)
F32 = jnp.float32
BF16 = jnp.bfloat16
MESH = pl.DeviceIdType.MESH


def dot(a, b, ca=1, cb=0):
    return lax.dot_general(a, b, (((ca,), (cb,)), ((), ())), preferred_element_type=F32)


def iota(shape, axis):
    return lax.broadcasted_iota(jnp.int32, shape, axis)


def pack_into(ref, tiles):
    low = iota((ROWS, 128), 0) % 8 < 4
    k0, k1, k2, k3 = tiles
    down = [pltpu.roll(t, 4, 0) for t in (k1, k3)]
    up = [pltpu.roll(t, ROWS - 4, 0) for t in (k0, k2)]
    even = [jnp.where(low, k0, down[0]), jnp.where(low, k2, down[1])]
    odd = [jnp.where(low, up[0], k1), jnp.where(low, up[1], k3)]
    halves = [jnp.concatenate([t.reshape(16, 8, 128) for t in pair], axis=1) for pair in (even, odd)]
    ref[...] = jnp.stack(halves, axis=1).reshape(NF, 16, 128).astype(ref.dtype)


def unpack(packed):
    packed = packed.reshape(16, 2, 16, 128)
    low = iota((ROWS, 128), 0) % 8 < 4
    e0 = packed[:, 0, 0:8].reshape(ROWS, 128)
    e1 = packed[:, 0, 8:16].reshape(ROWS, 128)
    o0 = packed[:, 1, 0:8].reshape(ROWS, 128)
    o1 = packed[:, 1, 8:16].reshape(ROWS, 128)
    down = [pltpu.roll(t, 4, 0) for t in (o0, o1)]
    up = [pltpu.roll(t, ROWS - 4, 0) for t in (e0, e1)]
    return (
        jnp.where(low, e0, down[0]),
        jnp.where(low, up[0], o0),
        jnp.where(low, e1, down[1]),
        jnp.where(low, up[1], o1),
    )


def split(x):
    high = x.astype(BF16).astype(F32)
    return high, x - high


def fold(x):
    n = x.shape[0] // 8
    tail = jnp.concatenate([x[:, 512:], jnp.zeros((n * 8, 128), x.dtype)], axis=1)
    return jnp.concatenate([x[:, :512].reshape(n, 8, 512), tail.reshape(n, 8, 512)], axis=1)


def unfold(x):
    n = x.shape[0]
    head = x[:, 0:8].reshape(n * 8, 512)
    tail = x[:, 8:16, 0:384].reshape(n * 8, 384)
    return jnp.concatenate([head, tail], axis=1)


def kernel(
    counts_ref,
    hidden_ref,
    embed_ref,
    target_ref,
    gain_ref,
    fc_hbm,
    gate_hbm,
    up_hbm,
    down_hbm,
    grad_fc_ref,
    grad_gain_ref,
    grad_gate_ref,
    grad_up_ref,
    grad_down_ref,
    fc_v,
    gate_v,
    up_v,
    down_v,
    fc_w,
    gate_w,
    up_w,
    down_w,
    a_src,
    a_dst,
    b1_src,
    b1_dst,
    b2_buf,
    d1_src,
    d1_dst,
    d2_buf,
    e1_src,
    e1_dst,
    e2_buf,
    f1_src,
    f1_dst,
    f2_buf,
    g1_src,
    g1_dst,
    g2_buf,
    load_sem,
    send_sem,
    recv_sem,
):
    z = lax.axis_index("roll")
    f = lax.axis_index("fsdp")

    def z_peer(i):
        offset = 8 + (i + 1) // 2 * (1 - 2 * (i % 2))
        return lax.rem(z + offset, NZ)

    def f_peer(i):
        return lax.rem(f + 1 + i, NF)

    loads = [
        pltpu.make_async_copy(a, b, load_sem.at[i])
        for i, (a, b) in enumerate(
            ((fc_hbm, fc_v), (gate_hbm, gate_v), (up_hbm, up_v), (down_hbm, down_v))
        )
    ]
    for load in loads:
        load.start()

    barrier = pltpu.get_barrier_semaphore()

    def greet_z(i, c):
        pl.semaphore_signal(barrier, inc=1, device_id=(z_peer(i), f), device_id_type=MESH)
        return c

    def greet_f(i, c):
        pl.semaphore_signal(barrier, inc=1, device_id=(z, f_peer(i)), device_id_type=MESH)
        return c

    lax.fori_loop(0, NZ - 1, greet_z, 0)
    lax.fori_loop(0, NF - 1, greet_f, 0)

    def send_z(phase, src, dst):
        def step(i, c):
            p = z_peer(i)
            pltpu.make_async_remote_copy(
                src_ref=dst.at[z] if src is None else src.at[p],
                dst_ref=dst.at[z],
                send_sem=send_sem.at[phase],
                recv_sem=recv_sem.at[phase],
                device_id=(p, f),
                device_id_type=MESH,
            ).start()
            return c

        lax.fori_loop(0, NZ - 1, step, 0)

    def send_f(phase, src, dst):
        def step(i, c):
            p = f_peer(i)
            pltpu.make_async_remote_copy(
                src_ref=dst.at[f] if src is None else src.at[p],
                dst_ref=dst.at[f],
                send_sem=send_sem.at[phase],
                recv_sem=recv_sem.at[phase],
                device_id=(z, p),
                device_id_type=MESH,
            ).start()
            return c

        lax.fori_loop(0, NF - 1, step, 0)

    def wait_z(sem, buf):
        part = buf.at[pl.ds(0, NZ - 1)]
        pltpu.make_async_copy(part, part, sem).wait()

    def wait_f(sem, buf):
        part = buf.at[pl.ds(0, NF - 1)]
        pltpu.make_async_copy(part, part, sem).wait()

    col = iota((160, DP), 1)
    row = iota((160, DP), 0)
    base = dot(embed_ref[...], (col == row).astype(F32).astype(BF16)) + dot(
        hidden_ref[...], (col == row + 160).astype(F32).astype(BF16)
    )
    base = jnp.where(iota((CAP, DP), 1) == DP - 1, counts_ref[0].astype(F32), base)
    wide = jnp.concatenate([target_ref[:, 640 * p : 640 * p + 640] for p in range(8)], axis=0)
    col = iota((640, 256), 1)
    row = iota((640, 256), 0)
    lane = col % 128 - 64
    wanted = row == col // 128 * DB + PIECE * f + lane
    pick = jnp.where((lane >= 0) & (lane < PIECE) & wanted, 1.0, 0.0).astype(BF16)
    pieces = dot(wide, pick)
    for p in range(NZ):
        piece = pieces[p // 2 * 16 : p // 2 * 16 + 16, p % 2 * 128 : p % 2 * 128 + 128]
        a_src[p, :, 0:256] = base[:, 0:256].astype(BF16)
        a_src[p, :, 256:384] = (base[:, 256:384] + piece).astype(BF16)
    a_dst[pl.ds(z, 1)] = a_src[pl.ds(z, 1)]

    pl.semaphore_wait(barrier, NZ - 1 + NF - 1)
    send_z(0, a_src, a_dst)

    fc_w[...] = jnp.zeros_like(fc_w)
    gate_w[...] = jnp.zeros_like(gate_w)
    up_w[...] = jnp.zeros_like(up_w)
    down_w[...] = jnp.zeros_like(down_w)
    for load in loads:
        load.wait()
    fc_w[0:DB, 0:DB] = fc_v[...]
    gate_w[0:DB, 0:FB] = gate_v[...]
    up_w[0:DB, 0:FB] = up_v[...]
    down_w[0:FB, 0:DB] = down_v[...]
    gain = jnp.concatenate(
        [gain_ref[:, 0:256], jnp.concatenate([gain_ref[:, 256:320], jnp.ones((1, 64), F32)], axis=1)],
        axis=1,
    )
    packed_row = iota((16, 128), 0)
    gain_p = jnp.where(
        packed_row < 4,
        gain[:, 0:128],
        jnp.where(packed_row < 8, gain[:, 128:256], gain[:, 256:384]),
    )
    wait_z(recv_sem.at[0], a_dst)

    slots = a_dst[...].reshape(NZ * CAP, DP)
    before = jnp.where(iota((256, 256), 1) // CAP < iota((256, 256), 0) // CAP, 1.0, 0.0).astype(BF16)
    start = dot(before, slots[:, 256:384])[:, 127:128] * (1.0 / CAP)
    count = slots[:, 256:384].astype(F32)[:, 127:128]
    place = (iota((256, ROWS), 0) % CAP).astype(F32)
    goes = iota((256, ROWS), 1).astype(F32) == start + place
    select = jnp.where((place < count) & goes, 1.0, 0.0).astype(BF16)
    live = dot(select, slots, 0, 0).astype(BF16)
    fc_part = dot(live, fc_w[...])
    none = jnp.zeros((ROWS, 128), F32)
    pack_into(b1_src, (fc_part[:, 0:128], fc_part[:, 128:256], fc_part[:, 256:384], none))
    mine_f = pl.ds(f, 1)
    b1_dst[mine_f] = b1_src[mine_f]
    send_f(1, b1_src, b1_dst)
    col = iota((128, DP), 1)
    row = iota((128, DP), 0) - 64
    lay = jnp.where((row >= 0) & (row < PIECE) & (col == PIECE * f + row), 1.0, 0.0).astype(BF16)
    target_part = dot(live[:, 256:384], lay)
    wait_f(recv_sem.at[1], b1_dst)

    def total_f(buf):
        return jnp.sum(buf[...].astype(F32), axis=0)

    mixed = total_f(b1_dst)
    b2_buf[mine_f] = (mixed * gain_p).astype(BF16).reshape(1, 16, 128)
    send_f(2, None, b2_buf)
    wait_f(recv_sem.at[2], b2_buf)

    h_tiles = unpack(b2_buf[...].astype(F32))
    h = jnp.concatenate(h_tiles[:3], axis=1)
    plain = h / gain
    squares = jnp.sum(plain * plain, axis=1, keepdims=True)
    h = h.astype(BF16)
    gate_part = dot(h, gate_w[...])
    up_part = dot(h, up_w[...])
    sq_high, sq_low = split(squares)
    lane = iota((ROWS, FP), 1)
    gate_part = jnp.where(lane == META, sq_high, jnp.where(lane == META + 1, sq_low, gate_part))
    d1_src[...] = jnp.concatenate(
        [gate_part.reshape(NZ, 8, FP), up_part.reshape(NZ, 8, FP)], axis=1
    ).astype(BF16)
    mine_z = pl.ds(z, 1)
    d1_dst[mine_z] = d1_src[mine_z]
    send_z(3, d1_src, d1_dst)
    wait_z(recv_sem.at[3], d1_dst)

    both = jnp.sum(d1_dst[...].astype(F32), axis=0)
    gate_sum, up_sum = both[0:8], both[8:16]
    lane8 = iota((8, FP), 1)
    square = jnp.sum(
        jnp.where((lane8 == META) | (lane8 == META + 1), gate_sum, 0.0), axis=1, keepdims=True
    )
    inverse = lax.rsqrt(square / D + EPS)
    real = lane8 < FB
    gate_pre = jnp.where(real, gate_sum * inverse, 0.0)
    up_pre = up_sum * inverse
    sig = jax.nn.sigmoid(gate_pre)
    act = gate_pre * sig * up_pre
    d2_buf[mine_z] = fold(act).astype(BF16)
    send_z(4, None, d2_buf)
    wait_z(recv_sem.at[4], d2_buf)

    act_all = unfold(d2_buf[...].astype(F32)).astype(BF16)
    down_part = dot(act_all, down_w[...]) - target_part
    pack_into(e1_src, (down_part[:, 0:128], down_part[:, 128:256], down_part[:, 256:384], none))
    e1_dst[mine_f] = e1_src[mine_f]
    send_f(5, e1_src, e1_dst)
    wait_f(recv_sem.at[5], e1_dst)

    loss_grad = (mixed + total_f(e1_dst)) * SCALE
    e2_buf[mine_f] = loss_grad.astype(BF16).reshape(1, 16, 128)
    send_f(6, None, e2_buf)
    wait_f(recv_sem.at[6], e2_buf)

    loss_all = jnp.concatenate(unpack(e2_buf[...].astype(F32))[:3], axis=1).astype(BF16)
    back_part = dot(loss_all, down_w[...], 1, 1)
    f1_src[...] = fold(back_part).astype(BF16)
    f1_dst[mine_z] = f1_src[mine_z]
    send_z(7, f1_src, f1_dst)
    grad_down_ref[...] = dot(act_all, loss_all, 0, 0)[0:FB, 0:DB]
    wait_z(recv_sem.at[7], f1_dst)

    back_act = unfold(jnp.sum(f1_dst[...].astype(F32), axis=0, keepdims=True))
    back_gate = back_act * up_pre * sig * (1.0 + gate_pre * (1.0 - sig))
    back_up = back_act * gate_pre * sig
    inner = inverse * inverse / D * jnp.sum(
        jnp.where(real, back_gate * gate_pre + back_up * up_pre, 0.0), axis=1, keepdims=True
    )
    in_high, in_low = split(inner)
    back_gate = jnp.where(real, back_gate * inverse, 0.0)
    back_gate = jnp.where(lane8 == META, in_high, jnp.where(lane8 == META + 1, in_low, back_gate))
    back_up = jnp.where(real, back_up * inverse, 0.0)
    f2_buf[mine_z] = jnp.concatenate([back_gate, back_up], axis=0).astype(BF16).reshape(1, 16, FP)
    send_z(8, None, f2_buf)
    wait_z(recv_sem.at[8], f2_buf)

    back_both = f2_buf[...].astype(F32)
    bg_all = back_both[:, 0:8].reshape(ROWS, FP)
    bu_all = back_both[:, 8:16].reshape(ROWS, FP).astype(BF16)
    lane = iota((ROWS, 128), 1) + 768
    inner_tile = jnp.where((lane == META) | (lane == META + 1), bg_all[:, 768:896], 0.0)
    bg_all = bg_all.astype(BF16)
    norm_part = dot(bg_all, gate_w[...], 1, 1) + dot(bu_all, up_w[...], 1, 1)
    pack_into(g1_src, (norm_part[:, 0:128], norm_part[:, 128:256], norm_part[:, 256:384], inner_tile))
    g1_dst[mine_f] = g1_src[mine_f]
    send_f(9, g1_src, g1_dst)
    grad_gate_ref[...] = dot(h, bg_all, 0, 0)[0:DB, 0:FB].astype(BF16)
    grad_up_ref[...] = dot(h, bu_all, 0, 0)[0:DB, 0:FB].astype(BF16)
    wait_f(recv_sem.at[9], g1_dst)

    back_norm = total_f(g1_dst)
    inner_col = jnp.sum(jnp.where(packed_row >= 12, back_norm, 0.0), axis=1, keepdims=True)
    inner_col = jnp.broadcast_to(inner_col, (16, 128))
    inner_all = pltpu.roll(inner_col, 4, 0) + pltpu.roll(inner_col, 8, 0) + pltpu.roll(inner_col, 12, 0)
    back_mix = loss_grad + gain_p * back_norm - mixed * inner_all
    terms = back_norm * mixed
    gain_sums = [
        jnp.sum(jnp.where(packed_row // 4 == k, terms, 0.0), axis=0, keepdims=True) for k in range(3)
    ]
    for k in range(3):
        back_mix = jnp.where(packed_row == 12 + k, gain_sums[k], back_mix)
    g2_buf[mine_f] = back_mix.astype(BF16).reshape(1, 16, 128)
    send_f(10, None, g2_buf)
    wait_f(recv_sem.at[10], g2_buf)

    mix_packed = g2_buf[...].astype(F32)
    mix_all = jnp.concatenate(unpack(mix_packed)[:3], axis=1).astype(BF16)
    grad_fc_ref[...] = dot(live, mix_all, 0, 0)[0:DB, 0:DB]
    gain_total = jnp.sum(mix_packed, axis=0)
    for k in range(3):
        grad_gain_ref[:, 128 * k : 128 * k + 128] = gain_total[12 + k : 13 + k]

    for phase, buf in ((0, a_dst), (3, d1_dst), (4, d2_buf), (7, f1_dst), (8, f2_buf)):
        wait_z(send_sem.at[phase], buf)
    for phase, buf in ((1, b1_dst), (2, b2_buf), (5, e1_dst), (6, e2_buf), (9, g1_dst), (10, g2_buf)):
        wait_f(send_sem.at[phase], buf)


def shards(
    hidden_rows,
    embed_rows,
    target_rows,
    counts,
    fc_weight,
    norm_gain,
    gate_weight,
    up_weight,
    down_weight,
):
    vmem = pl.BlockSpec(memory_space=pltpu.VMEM)
    hbm = pl.BlockSpec(memory_space=pl.ANY)
    xy = pltpu.VMEM((NF, 16, 128), BF16)
    grad_fc, grad_gain, grad_gate, grad_up, grad_down = pl.pallas_call(
        kernel,
        out_shape=(
            jax.ShapeDtypeStruct((DB, DB), F32),
            jax.ShapeDtypeStruct((1, DP), F32),
            jax.ShapeDtypeStruct((DB, FB), BF16),
            jax.ShapeDtypeStruct((DB, FB), BF16),
            jax.ShapeDtypeStruct((FB, DB), F32),
        ),
        in_specs=[pl.BlockSpec(memory_space=pltpu.SMEM)] + [vmem] * 4 + [hbm] * 4,
        out_specs=[vmem] * 5,
        scratch_shapes=[
            pltpu.VMEM((DB, DB), BF16),
            pltpu.VMEM((DB, FB), BF16),
            pltpu.VMEM((DB, FB), BF16),
            pltpu.VMEM((FB, DB), BF16),
            pltpu.VMEM((DP, DP), BF16),
            pltpu.VMEM((DP, FP), BF16),
            pltpu.VMEM((DP, FP), BF16),
            pltpu.VMEM((FP, DP), BF16),
            pltpu.VMEM((NZ, CAP, DP), BF16),
            pltpu.VMEM((NZ, CAP, DP), BF16),
            xy,
            xy,
            xy,
            pltpu.VMEM((NZ, 16, FP), BF16),
            pltpu.VMEM((NZ, 16, FP), BF16),
            pltpu.VMEM((NZ, 16, 512), BF16),
            xy,
            xy,
            xy,
            pltpu.VMEM((NZ, 16, 512), BF16),
            pltpu.VMEM((NZ, 16, 512), BF16),
            pltpu.VMEM((NZ, 16, FP), BF16),
            xy,
            xy,
            xy,
            pltpu.SemaphoreType.DMA((4,)),
            pltpu.SemaphoreType.DMA((11,)),
            pltpu.SemaphoreType.DMA((11,)),
        ],
        compiler_params=pltpu.CompilerParams(
            collective_id=0, has_side_effects=True, vmem_limit_bytes=48 << 20
        ),
        name="draft_layer",
    )(
        counts,
        hidden_rows,
        embed_rows,
        target_rows,
        norm_gain.reshape(1, DB),
        fc_weight.reshape(DB, DB),
        gate_weight,
        up_weight,
        down_weight,
    )
    return (
        grad_fc.reshape(2, DB // 2, DB),
        grad_gain[0, :DB],
        grad_gate,
        grad_up,
        grad_down,
    )


def solution(mesh):
    placed = (
        P("roll", "fsdp"),
        P("roll", "fsdp"),
        P("roll", None),
        P("roll"),
        P(None, "fsdp", "roll"),
        P("roll"),
        P("roll", "fsdp"),
        P("roll", "fsdp"),
        P("fsdp", "roll"),
    )
    return jax.shard_map(
        shards,
        mesh=mesh,
        in_specs=placed,
        out_specs=(
            P(None, "fsdp", "roll"),
            P("roll"),
            P("roll", "fsdp"),
            P("roll", "fsdp"),
            P("fsdp", "roll"),
        ),
        check_vma=False,
    )
```

```python
import math

import jax
import jax.numpy as jnp
from jax import lax
from jax.experimental import pallas as pl
from jax.experimental.pallas import tpu as pltpu
from jax.sharding import PartitionSpec as P

D = 5120
ROWS = 128
CAP = 16
NZ = 16
NF = 32
DB = 320
DP = 384
FB = 800
FP = 896
PIECE = DB // NF
META = 832
EPS = 1e-06
SCALE = 1.0 / math.sqrt(ROWS)
F32 = jnp.float32
BF16 = jnp.bfloat16
MESH = pl.DeviceIdType.MESH
Z_PEERS = (8, 4, -4, 3, -3, 2, -2, 1, -1)


def dot(a, b, ca=1, cb=0):
    return lax.dot_general(a, b, (((ca,), (cb,)), ((), ())), preferred_element_type=F32)


def iota(shape, axis):
    return lax.broadcasted_iota(jnp.int32, shape, axis)


def pack_into(ref, tiles):
    low = iota((ROWS, 128), 0) % 8 < 4
    k0, k1, k2, k3 = tiles
    down = [pltpu.roll(t, 4, 0) for t in (k1, k3)]
    up = [pltpu.roll(t, ROWS - 4, 0) for t in (k0, k2)]
    even = [jnp.where(low, k0, down[0]), jnp.where(low, k2, down[1])]
    odd = [jnp.where(low, up[0], k1), jnp.where(low, up[1], k3)]
    halves = [jnp.concatenate([t.reshape(16, 8, 128) for t in pair], axis=1) for pair in (even, odd)]
    ref[...] = jnp.stack(halves, axis=1).reshape(NF, 16, 128).astype(ref.dtype)


def unpack(packed):
    packed = packed.reshape(16, 2, 16, 128)
    low = iota((ROWS, 128), 0) % 8 < 4
    e0 = packed[:, 0, 0:8].reshape(ROWS, 128)
    e1 = packed[:, 0, 8:16].reshape(ROWS, 128)
    o0 = packed[:, 1, 0:8].reshape(ROWS, 128)
    o1 = packed[:, 1, 8:16].reshape(ROWS, 128)
    down = [pltpu.roll(t, 4, 0) for t in (o0, o1)]
    up = [pltpu.roll(t, ROWS - 4, 0) for t in (e0, e1)]
    return (
        jnp.where(low, e0, down[0]),
        jnp.where(low, up[0], o0),
        jnp.where(low, e1, down[1]),
        jnp.where(low, up[1], o1),
    )


def split(x):
    high = x.astype(BF16).astype(F32)
    return high, x - high


def fold(x):
    n = x.shape[0] // 8
    tail = jnp.concatenate([x[:, 512:], jnp.zeros((n * 8, 128), x.dtype)], axis=1)
    return jnp.concatenate([x[:, :512].reshape(n, 8, 512), tail.reshape(n, 8, 512)], axis=1)


def unfold(x):
    n = x.shape[0]
    head = x[:, 0:8].reshape(n * 8, 512)
    tail = x[:, 8:16, 0:384].reshape(n * 8, 384)
    return jnp.concatenate([head, tail], axis=1)


def seat(d):
    g = jnp.where(d == 0, 5, jnp.where(d == 1, 0, jnp.where(d == 15, 1, jnp.where(d == 2, 2, 3))))
    g = jnp.where(d == 8, 4, g)
    direct = 256 + 64 + PIECE * g
    up = 64 + PIECE * (d - 3)
    down = 128 + 64 + PIECE * (13 - d)
    return jnp.where((d >= 3) & (d <= 7), up, jnp.where((d >= 9) & (d <= 13), down, direct))


def kernel(
    counts_ref,
    hidden_hbm,
    embed_hbm,
    target_hbm,
    gain_hbm,
    fc_hbm,
    gate_hbm,
    up_hbm,
    down_hbm,
    grad_fc_ref,
    grad_gain_ref,
    grad_gate_ref,
    grad_up_ref,
    grad_down_ref,
    hidden_v,
    embed_v,
    target_v,
    gain_v,
    fc_v,
    gate_v,
    up_v,
    down_v,
    fc_w,
    gate_w,
    up_w,
    down_w,
    a_src,
    a_buf,
    b1_src,
    b1_dst,
    b2_buf,
    d1_src,
    d1_dst,
    d1_mid,
    d2_buf,
    e1_src,
    e1_dst,
    e2_buf,
    f1_src,
    f1_dst,
    f1_mid,
    f2_buf,
    g1_src,
    g1_dst,
    g2_buf,
    load_sem,
    send_sem,
    recv_sem,
):
    z = lax.axis_index("roll")
    f = lax.axis_index("fsdp")
    f_x, f_y, f_c = lax.div(f, 8), lax.rem(lax.div(f, 2), 4), lax.rem(f, 2)

    def z_at(offset):
        return lax.rem(z + (offset + NZ), NZ)

    def far_first(k):
        return lax.rem(10 - lax.div(k * (k + 1), 2), 4)

    def f_peer(i):
        j = lax.div(i, 2)
        x = lax.rem(f_x + far_first(lax.div(j, 4)), 4)
        y = lax.rem(f_y + far_first(lax.rem(j, 4)), 4)
        c = lax.rem(f_c + 1 + i, 2)
        return x * 8 + y * 2 + c

    loads = [
        pltpu.make_async_copy(a, b, load_sem.at[i])
        for i, (a, b) in enumerate(
            (
                (hidden_hbm, hidden_v),
                (embed_hbm, embed_v),
                (target_hbm, target_v),
                (gain_hbm, gain_v),
                (fc_hbm, fc_v),
                (gate_hbm, gate_v),
                (up_hbm, up_v),
                (down_hbm, down_v),
            )
        )
    ]
    for load in loads:
        load.start()

    barrier = pltpu.get_barrier_semaphore()

    def greet_f(i, c):
        pl.semaphore_signal(barrier, inc=1, device_id=(z, f_peer(i)), device_id_type=MESH)
        return c

    for d in Z_PEERS:
        pl.semaphore_signal(barrier, inc=1, device_id=(z_at(d), f), device_id_type=MESH)
    lax.fori_loop(0, NF - 1, greet_f, 0)

    def send_z(src, dst, d, phase, group):
        pltpu.make_async_remote_copy(
            src_ref=src,
            dst_ref=dst,
            send_sem=send_sem.at[phase],
            recv_sem=recv_sem.at[phase, group],
            device_id=(z_at(d), f),
            device_id_type=MESH,
        ).start()

    def settle(sem, buf, n):
        part = buf.at[pl.ds(0, n)]
        pltpu.make_async_copy(part, part, sem).wait()

    def gather_z(phase, buf, plus=None, minus=None):
        own = buf.at[z]
        send_z(own if plus is None else plus, own, 4, phase, 0)
        send_z(own if minus is None else minus, own, -4, phase, 1)
        for d in (8, 2, -2, 1, -1):
            send_z(own, own, d, phase, 2)

        def relay():
            settle(recv_sem.at[phase, 0], buf, 1)
            came = buf.at[z_at(-4)]
            for d in (3, 2, 1, -1):
                send_z(came, came, d, phase, 2)
            settle(recv_sem.at[phase, 1], buf, 1)
            came = buf.at[z_at(4)]
            for d in (-3, -2, -1, 1):
                send_z(came, came, d, phase, 2)

        return relay

    def wait_gather_z(phase, buf):
        settle(recv_sem.at[phase, 2], buf, 13)

    def reduce_z(phase, src, dst, mid):
        for at, d in ((3, 3), (2, 2), (1, 1), (0, -1)):
            send_z(src.at[z_at(d + 4)], dst.at[at], d, phase, 0)
            send_z(src.at[z_at(-d - 4)], dst.at[4 + at], -d, phase, 1)
        for at, d in ((10, 8), (11, 2), (12, -2), (13, 1), (14, -1)):
            send_z(src.at[z_at(d)], dst.at[at], d, phase, 2)
        for g, d in ((0, 4), (1, -4)):
            settle(recv_sem.at[phase, g], dst, 4)
            total = jnp.sum(dst[4 * g : 4 * g + 4].astype(F32), axis=0, keepdims=True)
            mid[g : g + 1] = (total + src[pl.ds(z_at(d), 1)].astype(F32)).astype(BF16)
            send_z(mid.at[g], dst.at[8 + g], d, phase, 2)

    def wait_reduce_z(phase, src, dst):
        settle(recv_sem.at[phase, 2], dst, 7)
        return jnp.sum(dst[8:15].astype(F32), axis=0) + src[pl.ds(z, 1)].astype(F32)[0]

    def send_f(phase, src, dst):
        def step(i, c):
            p = f_peer(i)
            pltpu.make_async_remote_copy(
                src_ref=dst.at[f] if src is None else src.at[p],
                dst_ref=dst.at[f],
                send_sem=send_sem.at[phase],
                recv_sem=recv_sem.at[phase, 0],
                device_id=(z, p),
                device_id_type=MESH,
            ).start()
            return c

        lax.fori_loop(0, NF - 1, step, 0)

    def wait_f(phase, buf):
        settle(recv_sem.at[phase, 0], buf, NF - 1)

    mine_z = pl.ds(z, 1)
    mine_f = pl.ds(f, 1)

    for load in loads[:4]:
        load.wait()
    col = iota((160, DP), 1)
    row = iota((160, DP), 0)
    base = dot(embed_v[...], (col == row).astype(F32).astype(BF16)) + dot(
        hidden_v[...], (col == row + 160).astype(F32).astype(BF16)
    )
    base = jnp.where(iota((CAP, DP), 1) == DP - 1, counts_ref[0].astype(F32), base)
    wide = jnp.concatenate([target_v[:, 640 * p : 640 * p + 640] for p in range(8)], axis=0)
    col = iota((640, 256), 1)
    row = iota((640, 256), 0)
    lane = col % 128
    wanted = row == col // 128 * DB + PIECE * f + lane
    pieces = dot(wide, jnp.where((lane < PIECE) & wanted, 1.0, 0.0).astype(BF16))
    line = [jnp.zeros((CAP, 128), F32), jnp.zeros((CAP, 128), F32)]
    for p in range(NZ):
        piece = pieces[p // 2 * 16 : p // 2 * 16 + 16, p % 2 * 128 : p % 2 * 128 + 128]
        shift = PIECE * p if p < 12 else PIECE * (p - 12)
        line[p // 12] += pltpu.roll(piece, shift, 1) if shift else piece
    line = jnp.concatenate(line, axis=1).astype(BF16)
    r = iota((256, 1), 0)
    r = jnp.where(r < 128, r, r - 8)
    receiver = (r * 205) >> 11
    goal = seat((receiver - z + NZ) % NZ) + r - receiver * PIECE
    goal = jnp.where(receiver < NZ, goal, -1)
    spread = jnp.where(goal == iota((256, 3 * 128), 1), 1.0, 0.0).astype(BF16)
    tails = dot(line, spread)
    for v in range(3):
        a_src[v, :, 0:256] = base[:, 0:256].astype(BF16)
        a_src[v, :, 256:384] = (base[:, 256:384] + tails[:, 128 * v : 128 * v + 128]).astype(BF16)
    a_buf[mine_z] = a_src[2:3]

    pl.semaphore_wait(barrier, len(Z_PEERS) + NF - 1)
    relay = gather_z(0, a_buf, a_src.at[0], a_src.at[1])

    fc_w[...] = jnp.zeros_like(fc_w)
    gate_w[...] = jnp.zeros_like(gate_w)
    up_w[...] = jnp.zeros_like(up_w)
    down_w[...] = jnp.zeros_like(down_w)
    for load in loads[4:]:
        load.wait()
    fc_w[0:DB, 0:DB] = fc_v[...]
    gate_w[0:DB, 0:FB] = gate_v[...]
    up_w[0:DB, 0:FB] = up_v[...]
    down_w[0:DB, 0:FB] = down_v[...]
    gain = gain_v[...].reshape(1, DB)
    gain = jnp.concatenate([gain, jnp.ones((1, DP - DB), F32)], axis=1)
    packed_row = iota((16, 128), 0)
    gain_p = jnp.where(
        packed_row < 4,
        gain[:, 0:128],
        jnp.where(packed_row < 8, gain[:, 128:256], gain[:, 256:384]),
    )
    relay()
    wait_gather_z(0, a_buf)

    slots = a_buf[...].reshape(NZ * CAP, DP)
    before = jnp.where(iota((256, 256), 1) // CAP < iota((256, 256), 0) // CAP, 1.0, 0.0).astype(BF16)
    start = dot(before, slots[:, 256:384])[:, 127:128] * (1.0 / CAP)
    count = slots[:, 256:384].astype(F32)[:, 127:128]
    place = (iota((256, ROWS), 0) % CAP).astype(F32)
    goes = iota((256, ROWS), 1).astype(F32) == start + place
    select = jnp.where((place < count) & goes, 1.0, 0.0).astype(BF16)
    group = seat((z - lax.div(iota((256, 1), 0), CAP) + NZ) % NZ) % 128
    lane = iota((256, 128), 1)
    meant = (lane >= group) & (lane < group + PIECE) | (lane < 64)
    tail = jnp.where(meant, slots[:, 256:384].astype(F32), 0.0).astype(BF16)
    slots = jnp.concatenate([slots[:, 0:256], tail], axis=1)
    live = dot(select, slots, 0, 0).astype(BF16)
    fc_part = dot(live, fc_w[...])
    none = jnp.zeros((ROWS, 128), F32)
    pack_into(b1_src, (fc_part[:, 0:128], fc_part[:, 128:256], fc_part[:, 256:384], none))
    b1_dst[mine_f] = b1_src[mine_f]
    send_f(1, b1_src, b1_dst)
    col = iota((128, DP), 1)
    row = iota((128, DP), 0) - 64
    inside = (row >= 0) & (row < 6 * PIECE)
    row = row - ((jnp.where(inside, row, 0) * 205) >> 11) * PIECE
    lay = jnp.where(inside & (col == PIECE * f + row), 1.0, 0.0).astype(BF16)
    target_part = dot(live[:, 256:384], lay)
    wait_f(1, b1_dst)

    def total_f(buf):
        return jnp.sum(buf[...].astype(F32), axis=0)

    mixed = total_f(b1_dst)
    b2_buf[mine_f] = (mixed * gain_p).astype(BF16).reshape(1, 16, 128)
    send_f(2, None, b2_buf)
    wait_f(2, b2_buf)

    h_tiles = unpack(b2_buf[...].astype(F32))
    h = jnp.concatenate(h_tiles[:3], axis=1)
    plain = h / gain
    squares = jnp.sum(plain * plain, axis=1, keepdims=True)
    h = h.astype(BF16)
    gate_part = dot(h, gate_w[...])
    up_part = dot(h, up_w[...])
    sq_high, sq_low = split(squares)
    lane = iota((ROWS, FP), 1)
    gate_part = jnp.where(lane == META, sq_high, jnp.where(lane == META + 1, sq_low, gate_part))
    d1_src[...] = jnp.concatenate(
        [gate_part.reshape(NZ, 8, FP), up_part.reshape(NZ, 8, FP)], axis=1
    ).astype(BF16)
    reduce_z(3, d1_src, d1_dst, d1_mid)
    both = wait_reduce_z(3, d1_src, d1_dst)
    gate_sum, up_sum = both[0:8], both[8:16]
    lane8 = iota((8, FP), 1)
    square = jnp.sum(
        jnp.where((lane8 == META) | (lane8 == META + 1), gate_sum, 0.0), axis=1, keepdims=True
    )
    inverse = lax.rsqrt(square / D + EPS)
    real = lane8 < FB
    gate_pre = jnp.where(real, gate_sum * inverse, 0.0)
    up_pre = up_sum * inverse
    sig = jax.nn.sigmoid(gate_pre)
    act = gate_pre * sig * up_pre
    d2_buf[mine_z] = fold(act).astype(BF16)
    gather_z(4, d2_buf)()
    wait_gather_z(4, d2_buf)

    act_all = unfold(d2_buf[...].astype(F32)).astype(BF16)
    down_part = dot(act_all, down_w[...], 1, 1) - target_part
    pack_into(e1_src, (down_part[:, 0:128], down_part[:, 128:256], down_part[:, 256:384], none))
    e1_dst[mine_f] = e1_src[mine_f]
    send_f(5, e1_src, e1_dst)
    wait_f(5, e1_dst)

    loss_grad = (mixed + total_f(e1_dst)) * SCALE
    e2_buf[mine_f] = loss_grad.astype(BF16).reshape(1, 16, 128)
    send_f(6, None, e2_buf)
    wait_f(6, e2_buf)

    loss_all = jnp.concatenate(unpack(e2_buf[...].astype(F32))[:3], axis=1).astype(BF16)
    back_part = dot(loss_all, down_w[...])
    f1_src[...] = fold(back_part).astype(BF16)
    reduce_z(7, f1_src, f1_dst, f1_mid)
    grad_down_ref[...] = dot(loss_all, act_all, 0, 0)[0:DB, 0:FB]
    back_act = wait_reduce_z(7, f1_src, f1_dst)
    back_act = unfold(back_act.reshape(1, 16, 512))
    back_gate = back_act * up_pre * sig * (1.0 + gate_pre * (1.0 - sig))
    back_up = back_act * gate_pre * sig
    inner = inverse * inverse / D * jnp.sum(
        jnp.where(real, back_gate * gate_pre + back_up * up_pre, 0.0), axis=1, keepdims=True
    )
    in_high, in_low = split(inner)
    back_gate = jnp.where(real, back_gate * inverse, 0.0)
    back_gate = jnp.where(lane8 == META, in_high, jnp.where(lane8 == META + 1, in_low, back_gate))
    back_up = jnp.where(real, back_up * inverse, 0.0)
    f2_buf[mine_z] = jnp.concatenate([back_gate, back_up], axis=0).astype(BF16).reshape(1, 16, FP)
    gather_z(8, f2_buf)()
    wait_gather_z(8, f2_buf)

    back_both = f2_buf[...].astype(F32)
    bg_all = back_both[:, 0:8].reshape(ROWS, FP)
    bu_all = back_both[:, 8:16].reshape(ROWS, FP).astype(BF16)
    lane = iota((ROWS, 128), 1) + 768
    inner_tile = jnp.where((lane == META) | (lane == META + 1), bg_all[:, 768:896], 0.0)
    bg_all = bg_all.astype(BF16)
    norm_part = dot(bg_all, gate_w[...], 1, 1) + dot(bu_all, up_w[...], 1, 1)
    pack_into(g1_src, (norm_part[:, 0:128], norm_part[:, 128:256], norm_part[:, 256:384], inner_tile))
    g1_dst[mine_f] = g1_src[mine_f]
    send_f(9, g1_src, g1_dst)
    grad_gate_ref[...] = dot(h, bg_all, 0, 0)[0:DB, 0:FB].astype(BF16)
    grad_up_ref[...] = dot(h, bu_all, 0, 0)[0:DB, 0:FB].astype(BF16)
    wait_f(9, g1_dst)

    back_norm = total_f(g1_dst)
    inner_col = jnp.sum(jnp.where(packed_row >= 12, back_norm, 0.0), axis=1, keepdims=True)
    inner_col = jnp.broadcast_to(inner_col, (16, 128))
    inner_all = pltpu.roll(inner_col, 4, 0) + pltpu.roll(inner_col, 8, 0) + pltpu.roll(inner_col, 12, 0)
    back_mix = loss_grad + gain_p * back_norm - mixed * inner_all
    terms = back_norm * mixed
    gain_sums = [
        jnp.sum(jnp.where(packed_row // 4 == k, terms, 0.0), axis=0, keepdims=True) for k in range(3)
    ]
    for k in range(3):
        back_mix = jnp.where(packed_row == 12 + k, gain_sums[k], back_mix)
    g2_buf[mine_f] = back_mix.astype(BF16).reshape(1, 16, 128)
    send_f(10, None, g2_buf)
    wait_f(10, g2_buf)

    mix_packed = g2_buf[...].astype(F32)
    mix_all = jnp.concatenate(unpack(mix_packed)[:3], axis=1).astype(BF16)
    grad_fc_ref[...] = dot(live, mix_all, 0, 0)[0:DB, 0:DB]
    gain_total = jnp.sum(mix_packed, axis=0)
    for k in range(3):
        grad_gain_ref[:, 128 * k : 128 * k + 128] = gain_total[12 + k : 13 + k]

    for phase, buf in ((0, a_buf), (3, d1_dst), (4, d2_buf), (7, f1_dst), (8, f2_buf)):
        settle(send_sem.at[phase], buf, NZ - 1)
    for phase, buf in ((1, b1_dst), (2, b2_buf), (5, e1_dst), (6, e2_buf), (9, g1_dst), (10, g2_buf)):
        settle(send_sem.at[phase], buf, NF - 1)


def store_kernel(*refs):
    sems = refs[10]
    copies = [pltpu.make_async_copy(refs[i], refs[5 + i], sems.at[i]) for i in range(5)]
    for copy in copies:
        copy.start()
    for copy in copies:
        copy.wait()


def shards(
    hidden_rows,
    embed_rows,
    target_rows,
    counts,
    fc_weight,
    norm_gain,
    gate_weight,
    up_weight,
    down_weight,
):
    vmem = pl.BlockSpec(memory_space=pltpu.VMEM)
    hbm = pl.BlockSpec(memory_space=pl.ANY)
    xy = pltpu.VMEM((NF, 16, 128), BF16)
    shapes = (
        jax.ShapeDtypeStruct((DB, DB), F32),
        jax.ShapeDtypeStruct((1, DP), F32),
        jax.ShapeDtypeStruct((DB, FB), BF16),
        jax.ShapeDtypeStruct((DB, FB), BF16),
        jax.ShapeDtypeStruct((DB, FB), F32),
    )
    found = pl.pallas_call(
        kernel,
        out_shape=shapes,
        in_specs=[pl.BlockSpec(memory_space=pltpu.SMEM)] + [hbm] * 8,
        out_specs=[vmem] * 5,
        scratch_shapes=[
            pltpu.VMEM((CAP, 160), BF16),
            pltpu.VMEM((CAP, 160), BF16),
            pltpu.VMEM((CAP, D), BF16),
            pltpu.VMEM((DB,), F32),
            pltpu.VMEM((DB, DB), BF16),
            pltpu.VMEM((DB, FB), BF16),
            pltpu.VMEM((DB, FB), BF16),
            pltpu.VMEM((DB, FB), BF16),
            pltpu.VMEM((DP, DP), BF16),
            pltpu.VMEM((DP, FP), BF16),
            pltpu.VMEM((DP, FP), BF16),
            pltpu.VMEM((DP, FP), BF16),
            pltpu.VMEM((3, CAP, DP), BF16),
            pltpu.VMEM((NZ, CAP, DP), BF16),
            xy,
            xy,
            xy,
            pltpu.VMEM((NZ, 16, FP), BF16),
            pltpu.VMEM((NZ - 1, 16, FP), BF16),
            pltpu.VMEM((2, 16, FP), BF16),
            pltpu.VMEM((NZ, 16, 512), BF16),
            xy,
            xy,
            xy,
            pltpu.VMEM((NZ, 16, 512), BF16),
            pltpu.VMEM((NZ - 1, 16, 512), BF16),
            pltpu.VMEM((2, 16, 512), BF16),
            pltpu.VMEM((NZ, 16, FP), BF16),
            xy,
            xy,
            xy,
            pltpu.SemaphoreType.DMA((8,)),
            pltpu.SemaphoreType.DMA((11,)),
            pltpu.SemaphoreType.DMA((11, 3)),
        ],
        compiler_params=pltpu.CompilerParams(
            collective_id=0, has_side_effects=True, vmem_limit_bytes=56 << 20
        ),
        name="draft_layer",
    )(
        counts,
        hidden_rows,
        embed_rows,
        target_rows,
        norm_gain,
        fc_weight.reshape(DB, DB),
        gate_weight,
        up_weight,
        down_weight.T,
    )
    grad_fc, grad_gain, grad_gate, grad_up, grad_down = pl.pallas_call(
        store_kernel,
        out_shape=shapes,
        in_specs=[vmem] * 5,
        out_specs=[hbm] * 5,
        scratch_shapes=[pltpu.SemaphoreType.DMA((5,))],
        name="store_results",
    )(*found)
    return (
        grad_fc.reshape(2, DB // 2, DB),
        grad_gain[0, :DB],
        grad_gate,
        grad_up,
        grad_down.T,
    )


def solution(mesh):
    placed = (
        P("roll", "fsdp"),
        P("roll", "fsdp"),
        P("roll", None),
        P("roll"),
        P(None, "fsdp", "roll"),
        P("roll"),
        P("roll", "fsdp"),
        P("roll", "fsdp"),
        P("fsdp", "roll"),
    )
    return jax.shard_map(
        shards,
        mesh=mesh,
        in_specs=placed,
        out_specs=(
            P(None, "fsdp", "roll"),
            P("roll"),
            P("roll", "fsdp"),
            P("roll", "fsdp"),
            P("fsdp", "roll"),
        ),
        check_vma=False,
    )
```

```python
import math

import jax
import jax.numpy as jnp
from jax import lax
from jax.experimental import pallas as pl
from jax.experimental.pallas import tpu as pltpu
from jax.sharding import PartitionSpec as P

D = 5120
ROWS = 128
CAP = 16
NZ = 16
NF = 32
DB = 320
DP = 384
FB = 800
FP = 896
PIECE = DB // NF
CUT = 384
META = 832
EPS = 1e-06
SCALE = 1.0 / math.sqrt(ROWS)
F32 = jnp.float32
BF16 = jnp.bfloat16
MESH = pl.DeviceIdType.MESH
Z_PEERS = (4, -4, 3, -3, 2, -2, 1, -1)


def dot(a, b, ca=1, cb=0):
    return lax.dot_general(a, b, (((ca,), (cb,)), ((), ())), preferred_element_type=F32)


def iota(shape, axis):
    return lax.broadcasted_iota(jnp.int32, shape, axis)


def pack_into(ref, tiles):
    low = iota((ROWS, 128), 0) % 8 < 4
    k0, k1, k2, k3 = tiles
    down = [pltpu.roll(t, 4, 0) for t in (k1, k3)]
    up = [pltpu.roll(t, ROWS - 4, 0) for t in (k0, k2)]
    even = [jnp.where(low, k0, down[0]), jnp.where(low, k2, down[1])]
    odd = [jnp.where(low, up[0], k1), jnp.where(low, up[1], k3)]
    halves = [jnp.concatenate([t.reshape(16, 8, 128) for t in pair], axis=1) for pair in (even, odd)]
    ref[...] = jnp.stack(halves, axis=1).reshape(NF, 16, 128).astype(ref.dtype)


def unpack(packed):
    packed = packed.reshape(16, 2, 16, 128)
    low = iota((ROWS, 128), 0) % 8 < 4
    e0 = packed[:, 0, 0:8].reshape(ROWS, 128)
    e1 = packed[:, 0, 8:16].reshape(ROWS, 128)
    o0 = packed[:, 1, 0:8].reshape(ROWS, 128)
    o1 = packed[:, 1, 8:16].reshape(ROWS, 128)
    down = [pltpu.roll(t, 4, 0) for t in (o0, o1)]
    up = [pltpu.roll(t, ROWS - 4, 0) for t in (e0, e1)]
    return (
        jnp.where(low, e0, down[0]),
        jnp.where(low, up[0], o0),
        jnp.where(low, e1, down[1]),
        jnp.where(low, up[1], o1),
    )


def split(x):
    high = x.astype(BF16).astype(F32)
    return high, x - high


def fold(x):
    n = x.shape[0] // 8
    tail = x[:, 256:]
    if tail.shape[1] < 256:
        tail = jnp.concatenate([tail, jnp.zeros((n * 8, 128), x.dtype)], axis=1)
    return jnp.concatenate([x[:, :256].reshape(n, 8, 256), tail.reshape(n, 8, 256)], axis=1)


def unfold(x, width):
    n = x.shape[0]
    head = x[:, 0:8].reshape(n * 8, 256)
    tail = x[:, 8:16, 0 : width - 256].reshape(n * 8, width - 256)
    return jnp.concatenate([head, tail], axis=1)


def twin(x, y):
    n, lanes = x.shape[0] // 8, x.shape[1]
    return jnp.concatenate([x.reshape(n, 8, lanes), y.reshape(n, 8, lanes)], axis=1)


def seat(d, side):
    g = jnp.where(d == 0, 4, jnp.where(d == 1, 0, jnp.where(d == 15, 1, jnp.where(d == 2, 2, 3))))
    direct = 256 + 64 + PIECE * g
    up = 64 + PIECE * (d - 3)
    down = 128 + 64 + PIECE * (13 - d)
    rises = (d >= 3) & (d <= 7) | (d == 8) & (side > 0)
    return jnp.where(rises, up, jnp.where((d >= 8) & (d <= 13), down, direct))


def kernel(
    counts_ref,
    hidden_hbm,
    embed_hbm,
    target_hbm,
    gain_hbm,
    fc_hbm,
    gate_hbm,
    up_hbm,
    down_hbm,
    grad_fc_hbm,
    grad_gain_hbm,
    grad_gate_hbm,
    grad_up_hbm,
    grad_down_hbm,
    hidden_v,
    embed_v,
    target_v,
    gain_v,
    fc_v,
    gate_v,
    up_v,
    down_v,
    fc_w,
    gate_w,
    up_w,
    down_w,
    a_src,
    a_buf,
    b1_src,
    b1_dst,
    b2_buf,
    d1a_src,
    d1a_dst,
    d1a_mid,
    d1b_src,
    d1b_dst,
    d1b_mid,
    d2a_buf,
    d2b_buf,
    e1_src,
    e1_dst,
    e2_buf,
    f1a_src,
    f1a_dst,
    f1a_mid,
    f1b_src,
    f1b_dst,
    f1b_mid,
    f2a_buf,
    f2b_buf,
    g1_src,
    g1_dst,
    g2_buf,
    grad_fc_v,
    grad_gain_v,
    grad_gate_v,
    grad_up_v,
    grad_down_v,
    load_sem,
    out_sem,
    send_sem,
    recv_sem,
):
    z = lax.axis_index("roll")
    f = lax.axis_index("fsdp")
    f_x, f_y, f_c = lax.div(f, 8), lax.rem(lax.div(f, 2), 4), lax.rem(f, 2)

    side = 1 - 2 * lax.rem(z, 2)

    def z_at(offset):
        return lax.rem(z + (offset + NZ), NZ)

    def far_first(k):
        return lax.rem(10 - lax.div(k * (k + 1), 2), 4)

    def f_peer(i):
        j = lax.div(i, 2)
        x = lax.rem(f_x + far_first(lax.div(j, 4)), 4)
        y = lax.rem(f_y + far_first(lax.rem(j, 4)), 4)
        c = lax.rem(f_c + 1 + i, 2)
        return x * 8 + y * 2 + c

    loads = [
        pltpu.make_async_copy(a, b, load_sem.at[i])
        for i, (a, b) in enumerate(
            (
                (hidden_hbm, hidden_v),
                (embed_hbm, embed_v),
                (target_hbm, target_v),
                (gain_hbm, gain_v),
                (fc_hbm, fc_v),
                (gate_hbm, gate_v),
                (up_hbm, up_v),
                (down_hbm, down_v),
            )
        )
    ]
    for load in loads:
        load.start()

    barrier = pltpu.get_barrier_semaphore()

    def greet_f(i, c):
        pl.semaphore_signal(barrier, inc=1, device_id=(z, f_peer(i)), device_id_type=MESH)
        return c

    for d in Z_PEERS:
        pl.semaphore_signal(barrier, inc=1, device_id=(z_at(d), f), device_id_type=MESH)
    lax.fori_loop(0, NF - 1, greet_f, 0)

    def send_z(src, dst, d, phase, group):
        pltpu.make_async_remote_copy(
            src_ref=src,
            dst_ref=dst,
            send_sem=send_sem.at[phase],
            recv_sem=recv_sem.at[phase, group],
            device_id=(z_at(d), f),
            device_id_type=MESH,
        ).start()

    def settle(sem, buf, n):
        part = buf.at[pl.ds(0, n)]
        pltpu.make_async_copy(part, part, sem).wait()

    def gather_start(phase, buf, plus=None, minus=None):
        own = buf.at[z]
        send_z(own if plus is None else plus, own, 4, phase, 0)
        send_z(own if minus is None else minus, own, -4, phase, 1)
        for d in (2, -2, 1, -1):
            send_z(own, own, d, phase, 2)

    def gather_relay(phase, buf):
        settle(recv_sem.at[phase, 0], buf, 1)
        settle(recv_sem.at[phase, 1], buf, 1)
        came = buf.at[z_at(-4 * side)]
        send_z(came, came, 4 * side, phase, 2)
        low, high = buf.at[z_at(-4)], buf.at[z_at(4)]
        for d in (3, 2, 1, -1):
            send_z(low, low, d, phase, 2)
            send_z(high, high, -d, phase, 2)

    def gather_end(phase, buf):
        settle(recv_sem.at[phase, 2], buf, 13)

    def reduce_start(phase, src, dst):
        for own, d, slot, group in (
            (8, -4 * side, 8, 3),
            (7, 3, 3, 0),
            (-7, -3, 7, 1),
            (6, 2, 2, 0),
            (-6, -2, 6, 1),
            (5, 1, 1, 0),
            (-5, -1, 5, 1),
            (3, -1, 0, 0),
            (-3, 1, 4, 1),
            (2, 2, 11, 2),
            (-2, -2, 12, 2),
            (1, 1, 13, 2),
            (-1, -1, 14, 2),
        ):
            send_z(src.at[z_at(own)], dst.at[slot], d, phase, group)

    def reduce_relay(phase, src, dst, mid):
        settle(recv_sem.at[phase, 3], dst, 1)
        far = dst[8:9].astype(F32)
        for g, d in ((0, 4), (1, -4)):
            settle(recv_sem.at[phase, g], dst, 4)
            total = jnp.sum(dst[4 * g : 4 * g + 4].astype(F32), axis=0, keepdims=True)
            total = total + src[pl.ds(z_at(d), 1)].astype(F32)
            total = total + jnp.where(side * d < 0, far, 0.0)
            mid[g : g + 1] = total.astype(BF16)
            send_z(mid.at[g], dst.at[9 + g], d, phase, 2)

    def reduce_end(phase, src, dst):
        settle(recv_sem.at[phase, 2], dst, 6)
        return jnp.sum(dst[9:15].astype(F32), axis=0) + src[pl.ds(z, 1)].astype(F32)[0]

    def send_f(phase, src, dst):
        def step(i, c):
            p = f_peer(i)
            pltpu.make_async_remote_copy(
                src_ref=dst.at[f] if src is None else src.at[p],
                dst_ref=dst.at[f],
                send_sem=send_sem.at[phase],
                recv_sem=recv_sem.at[phase, 0],
                device_id=(z, p),
                device_id_type=MESH,
            ).start()
            return c

        lax.fori_loop(0, NF - 1, step, 0)

    def wait_f(phase, buf):
        settle(recv_sem.at[phase, 0], buf, NF - 1)

    results = [
        pltpu.make_async_copy(a, b, out_sem.at[i])
        for i, (a, b) in enumerate(
            (
                (grad_fc_v, grad_fc_hbm),
                (grad_gain_v, grad_gain_hbm),
                (grad_gate_v, grad_gate_hbm),
                (grad_up_v, grad_up_hbm),
                (grad_down_v, grad_down_hbm),
            )
        )
    ]

    def leave(i):
        results[i].start()

    mine_z = pl.ds(z, 1)
    mine_f = pl.ds(f, 1)

    for load in loads[:4]:
        load.wait()
    col = iota((160, DP), 1)
    row = iota((160, DP), 0)
    base = dot(embed_v[...], (col == row).astype(F32).astype(BF16)) + dot(
        hidden_v[...], (col == row + 160).astype(F32).astype(BF16)
    )
    base = jnp.where(iota((CAP, DP), 1) == DP - 1, counts_ref[0].astype(F32), base)
    wide = jnp.concatenate([target_v[:, 640 * p : 640 * p + 640] for p in range(8)], axis=0)
    col = iota((640, 256), 1)
    row = iota((640, 256), 0)
    lane = col % 128
    wanted = row == col // 128 * DB + PIECE * f + lane
    pieces = dot(wide, jnp.where((lane < PIECE) & wanted, 1.0, 0.0).astype(BF16))
    line = [jnp.zeros((CAP, 128), F32), jnp.zeros((CAP, 128), F32)]
    for p in range(NZ):
        piece = pieces[p // 2 * 16 : p // 2 * 16 + 16, p % 2 * 128 : p % 2 * 128 + 128]
        shift = PIECE * p if p < 12 else PIECE * (p - 12)
        line[p // 12] += pltpu.roll(piece, shift, 1) if shift else piece
    line = jnp.concatenate(line, axis=1).astype(BF16)
    r = iota((256, 1), 0)
    r = jnp.where(r < 128, r, r - 8)
    receiver = (r * 205) >> 11
    goal = seat((receiver - z + NZ) % NZ, side) + r - receiver * PIECE
    goal = jnp.where(receiver < NZ, goal, -1)
    spread = jnp.where(goal == iota((256, 3 * 128), 1), 1.0, 0.0).astype(BF16)
    tails = dot(line, spread)
    for v in range(3):
        a_src[v, :, 0:256] = base[:, 0:256].astype(BF16)
        a_src[v, :, 256:384] = (base[:, 256:384] + tails[:, 128 * v : 128 * v + 128]).astype(BF16)
    a_buf[mine_z] = a_src[2:3]

    def prepare():
        fc_w[...] = jnp.zeros_like(fc_w)
        gate_w[...] = jnp.zeros_like(gate_w)
        up_w[...] = jnp.zeros_like(up_w)
        down_w[...] = jnp.zeros_like(down_w)
        for load in loads[4:]:
            load.wait()
        fc_w[0:DB, 0:DB] = fc_v[...]
        gate_w[0:DB, 0:FB] = gate_v[...]
        up_w[0:DB, 0:FB] = up_v[...]
        down_w[0:DB, 0:FB] = down_v[...]

    gain = gain_v[...].reshape(1, DB)
    gain = jnp.concatenate([gain, jnp.ones((1, DP - DB), F32)], axis=1)
    packed_row = iota((16, 128), 0)
    gain_p = jnp.where(
        packed_row < 4,
        gain[:, 0:128],
        jnp.where(packed_row < 8, gain[:, 128:256], gain[:, 256:384]),
    )
    pl.semaphore_wait(barrier, len(Z_PEERS) + NF - 1)
    gather_start(0, a_buf, a_src.at[0], a_src.at[1])
    prepare()
    gather_relay(0, a_buf)
    gather_end(0, a_buf)

    slots = a_buf[...].reshape(NZ * CAP, DP)
    before = jnp.where(iota((256, 256), 1) // CAP < iota((256, 256), 0) // CAP, 1.0, 0.0).astype(BF16)
    start = dot(before, slots[:, 256:384])[:, 127:128] * (1.0 / CAP)
    count = slots[:, 256:384].astype(F32)[:, 127:128]
    place = (iota((256, ROWS), 0) % CAP).astype(F32)
    goes = iota((256, ROWS), 1).astype(F32) == start + place
    select = jnp.where((place < count) & goes, 1.0, 0.0).astype(BF16)
    group = seat((z - lax.div(iota((256, 1), 0), CAP) + NZ) % NZ, side) % 128
    lane = iota((256, 128), 1)
    meant = (lane >= group) & (lane < group + PIECE) | (lane < 64)
    tail = jnp.where(meant, slots[:, 256:384].astype(F32), 0.0).astype(BF16)
    slots = jnp.concatenate([slots[:, 0:256], tail], axis=1)
    live = dot(select, slots, 0, 0).astype(BF16)
    fc_part = dot(live, fc_w[...])
    none = jnp.zeros((ROWS, 128), F32)
    pack_into(b1_src, (fc_part[:, 0:128], fc_part[:, 128:256], fc_part[:, 256:384], none))
    b1_dst[mine_f] = b1_src[mine_f]
    send_f(1, b1_src, b1_dst)
    col = iota((128, DP), 1)
    row = iota((128, DP), 0) - 64
    inside = (row >= 0) & (row < 6 * PIECE)
    row = row - ((jnp.where(inside, row, 0) * 205) >> 11) * PIECE
    lay = jnp.where(inside & (col == PIECE * f + row), 1.0, 0.0).astype(BF16)
    target_part = dot(live[:, 256:384], lay)
    wait_f(1, b1_dst)

    def total_f(buf):
        return jnp.sum(buf[...].astype(F32), axis=0)

    mixed = total_f(b1_dst)
    b2_buf[mine_f] = (mixed * gain_p).astype(BF16).reshape(1, 16, 128)
    send_f(2, None, b2_buf)
    wait_f(2, b2_buf)

    h_tiles = unpack(b2_buf[...].astype(F32))
    h = jnp.concatenate(h_tiles[:3], axis=1)
    plain = h / gain
    squares = jnp.sum(plain * plain, axis=1, keepdims=True)
    h = h.astype(BF16)
    gate_part = dot(h, gate_w[...])
    up_part = dot(h, up_w[...])
    sq_high, sq_low = split(squares)
    lane = iota((ROWS, FP), 1)
    gate_part = jnp.where(lane == META, sq_high, jnp.where(lane == META + 1, sq_low, gate_part))
    d1a_src[...] = twin(gate_part[:, CUT:], up_part[:, CUT:]).astype(BF16)
    reduce_start(3, d1a_src, d1a_dst)
    d1b_src[...] = twin(gate_part[:, :CUT], up_part[:, :CUT]).astype(BF16)
    reduce_start(4, d1b_src, d1b_dst)
    reduce_relay(3, d1a_src, d1a_dst, d1a_mid)
    reduce_relay(4, d1b_src, d1b_dst, d1b_mid)

    both_a = reduce_end(3, d1a_src, d1a_dst)
    lane_a = iota((8, FP - CUT), 1) + CUT
    real = lane_a < FB
    spare = (lane_a == META) | (lane_a == META + 1)
    square = jnp.sum(jnp.where(spare, both_a[0:8], 0.0), axis=1, keepdims=True)
    inverse = lax.rsqrt(square / D + EPS)
    gate_a = jnp.where(real, both_a[0:8] * inverse, 0.0)
    up_a = both_a[8:16] * inverse
    sig_a = jax.nn.sigmoid(gate_a)
    d2a_buf[mine_z] = fold(gate_a * sig_a * up_a).astype(BF16)
    gather_start(5, d2a_buf)

    both_b = reduce_end(4, d1b_src, d1b_dst)
    gate_b = both_b[0:8] * inverse
    up_b = both_b[8:16] * inverse
    sig_b = jax.nn.sigmoid(gate_b)
    d2b_buf[mine_z] = fold(gate_b * sig_b * up_b).astype(BF16)
    gather_start(6, d2b_buf)
    gather_relay(5, d2a_buf)
    gather_relay(6, d2b_buf)

    gather_end(5, d2a_buf)
    act_a = unfold(d2a_buf[...].astype(F32), FP - CUT).astype(BF16)
    down_part = dot(act_a, down_w[:, CUT:], 1, 1) - target_part
    gather_end(6, d2b_buf)
    act_b = unfold(d2b_buf[...].astype(F32), CUT).astype(BF16)
    down_part = down_part + dot(act_b, down_w[:, :CUT], 1, 1)
    pack_into(e1_src, (down_part[:, 0:128], down_part[:, 128:256], down_part[:, 256:384], none))
    e1_dst[mine_f] = e1_src[mine_f]
    send_f(7, e1_src, e1_dst)
    wait_f(7, e1_dst)

    loss_grad = (mixed + total_f(e1_dst)) * SCALE
    e2_buf[mine_f] = loss_grad.astype(BF16).reshape(1, 16, 128)
    send_f(8, None, e2_buf)
    wait_f(8, e2_buf)

    loss_all = jnp.concatenate(unpack(e2_buf[...].astype(F32))[:3], axis=1).astype(BF16)
    f1b_src[...] = fold(dot(loss_all, down_w[:, :CUT])).astype(BF16)
    reduce_start(9, f1b_src, f1b_dst)
    f1a_src[...] = fold(dot(loss_all, down_w[:, CUT:])).astype(BF16)
    reduce_start(10, f1a_src, f1a_dst)
    reduce_relay(9, f1b_src, f1b_dst, f1b_mid)
    reduce_relay(10, f1a_src, f1a_dst, f1a_mid)

    def back(back_act, gate_pre, up_pre, sig):
        back_gate = back_act * up_pre * sig * (1.0 + gate_pre * (1.0 - sig))
        back_up = back_act * gate_pre * sig
        return back_gate, back_up, back_gate * gate_pre + back_up * up_pre

    back_b = unfold(reduce_end(9, f1b_src, f1b_dst).reshape(1, 16, 256), CUT)
    bg, bu, terms_b = back(back_b, gate_b, up_b, sig_b)
    f2b_buf[mine_z] = twin(bg * inverse, bu * inverse).astype(BF16)
    gather_start(11, f2b_buf)

    back_a = unfold(reduce_end(10, f1a_src, f1a_dst).reshape(1, 16, 256), FP - CUT)
    bg, bu, terms_a = back(back_a, gate_a, up_a, sig_a)
    inner = jnp.sum(jnp.where(real, terms_a, 0.0), axis=1, keepdims=True)
    inner = inverse * inverse / D * (inner + jnp.sum(terms_b, axis=1, keepdims=True))
    in_high, in_low = split(inner)
    bg = jnp.where(real, bg * inverse, 0.0)
    bg = jnp.where(lane_a == META, in_high, jnp.where(lane_a == META + 1, in_low, bg))
    bu = jnp.where(real, bu * inverse, 0.0)
    f2a_buf[mine_z] = twin(bg, bu).astype(BF16)
    gather_start(12, f2a_buf)
    gather_relay(11, f2b_buf)
    gather_relay(12, f2a_buf)
    grad_down_v[:, 0:CUT] = dot(loss_all, act_b, 0, 0)[0:DB]
    grad_down_v[:, CUT:FB] = dot(loss_all, act_a, 0, 0)[0:DB, 0 : FB - CUT]
    leave(4)

    gather_end(11, f2b_buf)
    back_both = f2b_buf[...].astype(F32)
    bg_b = back_both[:, 0:8].reshape(ROWS, CUT).astype(BF16)
    bu_b = back_both[:, 8:16].reshape(ROWS, CUT).astype(BF16)
    norm_part = dot(bg_b, gate_w[:, :CUT], 1, 1) + dot(bu_b, up_w[:, :CUT], 1, 1)
    gather_end(12, f2a_buf)
    back_both = f2a_buf[...].astype(F32)
    bg_a = back_both[:, 0:8].reshape(ROWS, FP - CUT)
    bu_a = back_both[:, 8:16].reshape(ROWS, FP - CUT).astype(BF16)
    lane = iota((ROWS, 128), 1) + 768
    inner_tile = jnp.where((lane == META) | (lane == META + 1), bg_a[:, 768 - CUT :], 0.0)
    bg_a = bg_a.astype(BF16)
    norm_part = norm_part + dot(bg_a, gate_w[:, CUT:], 1, 1) + dot(bu_a, up_w[:, CUT:], 1, 1)
    pack_into(g1_src, (norm_part[:, 0:128], norm_part[:, 128:256], norm_part[:, 256:384], inner_tile))
    g1_dst[mine_f] = g1_src[mine_f]
    send_f(13, g1_src, g1_dst)
    for grad, back_a, back_b in ((grad_gate_v, bg_a, bg_b), (grad_up_v, bu_a, bu_b)):
        grad[:, 0:CUT] = dot(h, back_b, 0, 0)[0:DB].astype(BF16)
        grad[:, CUT:FB] = dot(h, back_a, 0, 0)[0:DB, 0 : FB - CUT].astype(BF16)
    leave(2)
    leave(3)
    wait_f(13, g1_dst)

    back_norm = total_f(g1_dst)
    inner_col = jnp.sum(jnp.where(packed_row >= 12, back_norm, 0.0), axis=1, keepdims=True)
    inner_col = jnp.broadcast_to(inner_col, (16, 128))
    inner_all = pltpu.roll(inner_col, 4, 0) + pltpu.roll(inner_col, 8, 0) + pltpu.roll(inner_col, 12, 0)
    back_mix = loss_grad + gain_p * back_norm - mixed * inner_all
    terms = back_norm * mixed
    gain_sums = [
        jnp.sum(jnp.where(packed_row // 4 == k, terms, 0.0), axis=0, keepdims=True) for k in range(3)
    ]
    for k in range(3):
        back_mix = jnp.where(packed_row == 12 + k, gain_sums[k], back_mix)
    g2_buf[mine_f] = back_mix.astype(BF16).reshape(1, 16, 128)
    send_f(14, None, g2_buf)
    wait_f(14, g2_buf)

    mix_packed = g2_buf[...].astype(F32)
    mix_all = jnp.concatenate(unpack(mix_packed)[:3], axis=1).astype(BF16)
    grad_fc_v[...] = dot(live, mix_all, 0, 0)[0:DB, 0:DB]
    leave(0)
    gain_total = jnp.sum(mix_packed, axis=0)
    gain_line = jnp.concatenate([gain_total[12 + k : 13 + k] for k in range(3)], axis=1)
    grad_gain_v[...] = gain_line[:, 0:DB].reshape(DB)
    leave(1)

    for phase, buf in (
        (0, a_buf),
        (3, d1a_dst),
        (4, d1b_dst),
        (5, d2a_buf),
        (6, d2b_buf),
        (9, f1b_dst),
        (10, f1a_dst),
        (11, f2b_buf),
        (12, f2a_buf),
    ):
        settle(send_sem.at[phase], buf, NZ - 1)
    for phase, buf in ((1, b1_dst), (2, b2_buf), (7, e1_dst), (8, e2_buf), (13, g1_dst), (14, g2_buf)):
        settle(send_sem.at[phase], buf, NF - 1)
    for result in results:
        result.wait()


def store_kernel(*refs):
    sources, targets, held = refs[0:5], refs[5:10], refs[10:15]
    in_sem, out_sem = refs[15:17]
    order = (4, 2, 3, 0, 1)
    loads = {i: pltpu.make_async_copy(sources[i], held[i], in_sem.at[i]) for i in order}
    stores = {i: pltpu.make_async_copy(held[i], targets[i], out_sem.at[i]) for i in order}
    for i in order:
        loads[i].start()
    for i in order:
        loads[i].wait()
        stores[i].start()
    for i in order:
        stores[i].wait()


def shards(
    hidden_rows,
    embed_rows,
    target_rows,
    counts,
    fc_weight,
    norm_gain,
    gate_weight,
    up_weight,
    down_weight,
):
    vmem = pl.BlockSpec(memory_space=pltpu.VMEM)
    hbm = pl.BlockSpec(memory_space=pl.ANY)
    xy = pltpu.VMEM((NF, 16, 128), BF16)
    shapes = (
        jax.ShapeDtypeStruct((DB, DB), F32),
        jax.ShapeDtypeStruct((DB,), F32),
        jax.ShapeDtypeStruct((DB, FB), BF16),
        jax.ShapeDtypeStruct((DB, FB), BF16),
        jax.ShapeDtypeStruct((DB, FB), F32),
    )
    found = pl.pallas_call(
        kernel,
        out_shape=shapes,
        in_specs=[pl.BlockSpec(memory_space=pltpu.SMEM)] + [hbm] * 8,
        out_specs=[hbm] * 5,
        scratch_shapes=[
            pltpu.VMEM((CAP, 160), BF16),
            pltpu.VMEM((CAP, 160), BF16),
            pltpu.VMEM((CAP, D), BF16),
            pltpu.VMEM((DB,), F32),
            pltpu.VMEM((DB, DB), BF16),
            pltpu.VMEM((DB, FB), BF16),
            pltpu.VMEM((DB, FB), BF16),
            pltpu.VMEM((DB, FB), BF16),
            pltpu.VMEM((DP, DP), BF16),
            pltpu.VMEM((DP, FP), BF16),
            pltpu.VMEM((DP, FP), BF16),
            pltpu.VMEM((DP, FP), BF16),
            pltpu.VMEM((3, CAP, DP), BF16),
            pltpu.VMEM((NZ, CAP, DP), BF16),
            xy,
            xy,
            xy,
            pltpu.VMEM((NZ, 16, FP - CUT), BF16),
            pltpu.VMEM((NZ - 1, 16, FP - CUT), BF16),
            pltpu.VMEM((2, 16, FP - CUT), BF16),
            pltpu.VMEM((NZ, 16, CUT), BF16),
            pltpu.VMEM((NZ - 1, 16, CUT), BF16),
            pltpu.VMEM((2, 16, CUT), BF16),
            pltpu.VMEM((NZ, 16, 256), BF16),
            pltpu.VMEM((NZ, 16, 256), BF16),
            xy,
            xy,
            xy,
            pltpu.VMEM((NZ, 16, 256), BF16),
            pltpu.VMEM((NZ - 1, 16, 256), BF16),
            pltpu.VMEM((2, 16, 256), BF16),
            pltpu.VMEM((NZ, 16, 256), BF16),
            pltpu.VMEM((NZ - 1, 16, 256), BF16),
            pltpu.VMEM((2, 16, 256), BF16),
            pltpu.VMEM((NZ, 16, FP - CUT), BF16),
            pltpu.VMEM((NZ, 16, CUT), BF16),
            xy,
            xy,
            xy,
            pltpu.VMEM((DB, DB), F32),
            pltpu.VMEM((DB,), F32),
            pltpu.VMEM((DB, FB), BF16),
            pltpu.VMEM((DB, FB), BF16),
            pltpu.VMEM((DB, FB), F32),
            pltpu.SemaphoreType.DMA((8,)),
            pltpu.SemaphoreType.DMA((5,)),
            pltpu.SemaphoreType.DMA((15,)),
            pltpu.SemaphoreType.DMA((15, 4)),
        ],
        compiler_params=pltpu.CompilerParams(
            collective_id=0, has_side_effects=True, vmem_limit_bytes=56 << 20
        ),
        name="draft_layer",
    )(
        counts,
        hidden_rows,
        embed_rows,
        target_rows,
        norm_gain,
        fc_weight.reshape(DB, DB),
        gate_weight,
        up_weight,
        down_weight.T,
    )
    grad_fc, grad_gain, grad_gate, grad_up, grad_down = pl.pallas_call(
        store_kernel,
        out_shape=shapes,
        in_specs=[hbm] * 5,
        out_specs=[hbm] * 5,
        scratch_shapes=[pltpu.VMEM(shape.shape, shape.dtype) for shape in shapes]
        + [pltpu.SemaphoreType.DMA((5,)), pltpu.SemaphoreType.DMA((5,))],
        name="store_results",
    )(*found)
    return (
        grad_fc.reshape(2, DB // 2, DB),
        grad_gain,
        grad_gate,
        grad_up,
        grad_down.T,
    )


def solution(mesh):
    placed = (
        P("roll", "fsdp"),
        P("roll", "fsdp"),
        P("roll", None),
        P("roll"),
        P(None, "fsdp", "roll"),
        P("roll"),
        P("roll", "fsdp"),
        P("roll", "fsdp"),
        P("fsdp", "roll"),
    )
    return jax.shard_map(
        shards,
        mesh=mesh,
        in_specs=placed,
        out_specs=(
            P(None, "fsdp", "roll"),
            P("roll"),
            P("roll", "fsdp"),
            P("roll", "fsdp"),
            P("fsdp", "roll"),
        ),
        check_vma=False,
    )
```

```python
import math

import jax
import jax.numpy as jnp
from jax import lax
from jax.experimental import pallas as pl
from jax.experimental.pallas import tpu as pltpu
from jax.sharding import PartitionSpec as P

D = 5120
ROWS = 128
CAP = 16
NZ = 16
NF = 32
DB = 320
DP = 384
FB = 800
FP = 896
PIECE = DB // NF
CUT = 384
META = 832
EPS = 1e-06
F_ORDER = sorted(
    ((x, y, c) for x in range(4) for y in range(4) for c in range(2) if x + y + c),
    key=lambda at: -min(at[0], 4 - at[0]) - min(at[1], 4 - at[1]),
)
SCALE = 1.0 / math.sqrt(ROWS)
F32 = jnp.float32
BF16 = jnp.bfloat16
MESH = pl.DeviceIdType.MESH
Z_PEERS = (4, -4, 3, -3, 2, -2, 1, -1)


def dot(a, b, ca=1, cb=0):
    return lax.dot_general(a, b, (((ca,), (cb,)), ((), ())), preferred_element_type=F32)


def iota(shape, axis):
    return lax.broadcasted_iota(jnp.int32, shape, axis)


def pack_into(ref, tiles):
    low = iota((ROWS, 128), 0) % 8 < 4
    k0, k1, k2, k3 = tiles
    down = [pltpu.roll(t, 4, 0) for t in (k1, k3)]
    up = [pltpu.roll(t, ROWS - 4, 0) for t in (k0, k2)]
    even = [jnp.where(low, k0, down[0]), jnp.where(low, k2, down[1])]
    odd = [jnp.where(low, up[0], k1), jnp.where(low, up[1], k3)]
    halves = [jnp.concatenate([t.reshape(16, 8, 128) for t in pair], axis=1) for pair in (even, odd)]
    ref[...] = jnp.stack(halves, axis=1).reshape(NF, 16, 128).astype(ref.dtype)


def unpack(packed):
    packed = packed.reshape(16, 2, 16, 128)
    low = iota((ROWS, 128), 0) % 8 < 4
    e0 = packed[:, 0, 0:8].reshape(ROWS, 128)
    e1 = packed[:, 0, 8:16].reshape(ROWS, 128)
    o0 = packed[:, 1, 0:8].reshape(ROWS, 128)
    o1 = packed[:, 1, 8:16].reshape(ROWS, 128)
    down = [pltpu.roll(t, 4, 0) for t in (o0, o1)]
    up = [pltpu.roll(t, ROWS - 4, 0) for t in (e0, e1)]
    return (
        jnp.where(low, e0, down[0]),
        jnp.where(low, up[0], o0),
        jnp.where(low, e1, down[1]),
        jnp.where(low, up[1], o1),
    )


def split(x):
    high = x.astype(BF16).astype(F32)
    return high, x - high


def fold(x):
    n = x.shape[0] // 8
    tail = x[:, 256:]
    if tail.shape[1] < 256:
        tail = jnp.concatenate([tail, jnp.zeros((n * 8, 128), x.dtype)], axis=1)
    return jnp.concatenate([x[:, :256].reshape(n, 8, 256), tail.reshape(n, 8, 256)], axis=1)


def unfold(x, width):
    n = x.shape[0]
    head = x[:, 0:8].reshape(n * 8, 256)
    tail = x[:, 8:16, 0 : width - 256].reshape(n * 8, width - 256)
    return jnp.concatenate([head, tail], axis=1)


def twin(x, y):
    n, lanes = x.shape[0] // 8, x.shape[1]
    return jnp.concatenate([x.reshape(n, 8, lanes), y.reshape(n, 8, lanes)], axis=1)


def seat(d, side):
    g = jnp.where(d == 0, 4, jnp.where(d == 1, 0, jnp.where(d == 15, 1, jnp.where(d == 2, 2, 3))))
    direct = 256 + 64 + PIECE * g
    up = 64 + PIECE * (d - 3)
    down = 128 + 64 + PIECE * (13 - d)
    rises = (d >= 3) & (d <= 7) | (d == 8) & (side > 0)
    return jnp.where(rises, up, jnp.where((d >= 8) & (d <= 13), down, direct))


def kernel(
    counts_ref,
    hidden_hbm,
    embed_hbm,
    target_hbm,
    gain_hbm,
    fc_hbm,
    gate_hbm,
    up_hbm,
    down_hbm,
    grad_fc_hbm,
    grad_gain_hbm,
    grad_gate_hbm,
    grad_up_hbm,
    grad_down_hbm,
    hidden_v,
    embed_v,
    target_v,
    gain_v,
    fc_v,
    gate_v,
    up_v,
    down_v,
    fc_w,
    gate_w,
    up_w,
    down_w,
    a_src,
    a_buf,
    b1_src,
    b1_dst,
    b2_buf,
    d1a_src,
    d1a_dst,
    d1a_mid,
    d1b_src,
    d1b_dst,
    d1b_mid,
    d2a_buf,
    d2b_buf,
    e1_src,
    e1_dst,
    e2_buf,
    f1a_src,
    f1a_dst,
    f1a_mid,
    f1b_src,
    f1b_dst,
    f1b_mid,
    f2a_buf,
    f2b_buf,
    g1_src,
    g1_dst,
    g2_buf,
    grad_fc_v,
    grad_gain_v,
    grad_gate_v,
    grad_up_v,
    grad_down_v,
    load_sem,
    out_sem,
    send_sem,
    recv_sem,
):
    z = lax.axis_index("roll")
    f = lax.axis_index("fsdp")
    f_x, f_y, f_c = lax.div(f, 8), lax.rem(lax.div(f, 2), 4), lax.rem(f, 2)

    side = 1 - 2 * lax.rem(z, 2)

    def z_at(offset):
        return lax.rem(z + (offset + NZ), NZ)

    def f_peer(i):
        dx, dy, dc = F_ORDER[i]
        x = lax.rem(f_x + dx, 4)
        y = lax.rem(f_y + dy, 4)
        c = f_c if dc == 0 else 1 - f_c
        return x * 8 + y * 2 + c

    loads = [
        pltpu.make_async_copy(a, b, load_sem.at[i])
        for i, (a, b) in enumerate(
            (
                (hidden_hbm, hidden_v),
                (embed_hbm, embed_v),
                (target_hbm, target_v),
                (gain_hbm, gain_v),
                (fc_hbm, fc_v),
                (gate_hbm, gate_v),
                (up_hbm, up_v),
                (down_hbm, down_v),
            )
        )
    ]
    for load in loads:
        load.start()

    barrier = pltpu.get_barrier_semaphore()

    def greet_f(i, c):
        pl.semaphore_signal(barrier, inc=1, device_id=(z, f_peer(i)), device_id_type=MESH)
        return c

    for d in Z_PEERS:
        pl.semaphore_signal(barrier, inc=1, device_id=(z_at(d), f), device_id_type=MESH)
    for i in range(NF - 1):
        greet_f(i, 0)

    def send_z(src, dst, d, phase, group):
        pltpu.make_async_remote_copy(
            src_ref=src,
            dst_ref=dst,
            send_sem=send_sem.at[phase],
            recv_sem=recv_sem.at[phase, group],
            device_id=(z_at(d), f),
            device_id_type=MESH,
        ).start()

    def settle(sem, buf, n):
        part = buf.at[pl.ds(0, n)]
        pltpu.make_async_copy(part, part, sem).wait()

    def gather_start(phase, buf, plus=None, minus=None):
        own = buf.at[z]
        send_z(own if plus is None else plus, own, 4, phase, 0)
        send_z(own if minus is None else minus, own, -4, phase, 1)
        for d in (2, -2, 1, -1):
            send_z(own, own, d, phase, 2)

    def gather_relay(phase, buf):
        settle(recv_sem.at[phase, 0], buf, 1)
        settle(recv_sem.at[phase, 1], buf, 1)
        came = buf.at[z_at(-4 * side)]
        send_z(came, came, 4 * side, phase, 2)
        low, high = buf.at[z_at(-4)], buf.at[z_at(4)]
        for d in (3, 2, 1, -1):
            send_z(low, low, d, phase, 2)
            send_z(high, high, -d, phase, 2)

    def gather_end(phase, buf):
        settle(recv_sem.at[phase, 2], buf, 13)

    def reduce_start(phase, src, dst):
        for own, d, slot, group in (
            (8, -4 * side, 8, 3),
            (7, 3, 3, 0),
            (-7, -3, 7, 1),
            (6, 2, 2, 0),
            (-6, -2, 6, 1),
            (5, 1, 1, 0),
            (-5, -1, 5, 1),
            (3, -1, 0, 0),
            (-3, 1, 4, 1),
        ):
            send_z(src.at[z_at(own)], dst.at[slot], d, phase, group)

    def reduce_near(phase, src, dst):
        for d, slot in ((2, 11), (-2, 12), (1, 13), (-1, 14)):
            send_z(src.at[z_at(d)], dst.at[slot], d, phase, 2)

    def reduce_relay(phase, src, dst, mid):
        settle(recv_sem.at[phase, 3], dst, 1)
        far = dst[8:9].astype(F32)
        for g, d in ((0, 4), (1, -4)):
            settle(recv_sem.at[phase, g], dst, 4)
            total = jnp.sum(dst[4 * g : 4 * g + 4].astype(F32), axis=0, keepdims=True)
            total = total + src[pl.ds(z_at(d), 1)].astype(F32)
            total = total + jnp.where(side * d < 0, far, 0.0)
            mid[g : g + 1] = total.astype(BF16)
            send_z(mid.at[g], dst.at[9 + g], d, phase, 2)

    def reduce_end(phase, src, dst):
        settle(recv_sem.at[phase, 2], dst, 6)
        return jnp.sum(dst[9:15].astype(F32), axis=0) + src[pl.ds(z, 1)].astype(F32)[0]

    def send_f(phase, src, dst):
        def step(i, c):
            p = f_peer(i)
            pltpu.make_async_remote_copy(
                src_ref=dst.at[f] if src is None else src.at[p],
                dst_ref=dst.at[f],
                send_sem=send_sem.at[phase],
                recv_sem=recv_sem.at[phase, 0],
                device_id=(z, p),
                device_id_type=MESH,
            ).start()
            return c

        for i in range(NF - 1):
            step(i, 0)

    def wait_f(phase, buf):
        settle(recv_sem.at[phase, 0], buf, NF - 1)

    results = [
        pltpu.make_async_copy(a, b, out_sem.at[i])
        for i, (a, b) in enumerate(
            (
                (grad_fc_v, grad_fc_hbm),
                (grad_gain_v, grad_gain_hbm),
                (grad_gate_v, grad_gate_hbm),
                (grad_up_v, grad_up_hbm),
                (grad_down_v, grad_down_hbm),
            )
        )
    ]

    def leave(i):
        results[i].start()

    mine_z = pl.ds(z, 1)
    mine_f = pl.ds(f, 1)

    for load in loads[:4]:
        load.wait()
    col = iota((160, DP), 1)
    row = iota((160, DP), 0)
    base = dot(embed_v[...], (col == row).astype(F32).astype(BF16)) + dot(
        hidden_v[...], (col == row + 160).astype(F32).astype(BF16)
    )
    base = jnp.where(iota((CAP, DP), 1) == DP - 1, counts_ref[0].astype(F32), base)
    wide = jnp.concatenate([target_v[:, 640 * p : 640 * p + 640] for p in range(8)], axis=0)
    col = iota((640, 256), 1)
    row = iota((640, 256), 0)
    lane = col % 128
    wanted = row == col // 128 * DB + PIECE * f + lane
    pieces = dot(wide, jnp.where((lane < PIECE) & wanted, 1.0, 0.0).astype(BF16))
    line = [jnp.zeros((CAP, 128), F32), jnp.zeros((CAP, 128), F32)]
    for p in range(NZ):
        piece = pieces[p // 2 * 16 : p // 2 * 16 + 16, p % 2 * 128 : p % 2 * 128 + 128]
        shift = PIECE * p if p < 12 else PIECE * (p - 12)
        line[p // 12] += pltpu.roll(piece, shift, 1) if shift else piece
    line = jnp.concatenate(line, axis=1).astype(BF16)
    r = iota((256, 1), 0)
    r = jnp.where(r < 128, r, r - 8)
    receiver = (r * 205) >> 11
    goal = seat((receiver - z + NZ) % NZ, side) + r - receiver * PIECE
    goal = jnp.where(receiver < NZ, goal, -1)
    spread = jnp.where(goal == iota((256, 3 * 128), 1), 1.0, 0.0).astype(BF16)
    tails = dot(line, spread)
    for v in range(3):
        a_src[v, :, 0:256] = base[:, 0:256].astype(BF16)
        a_src[v, :, 256:384] = (base[:, 256:384] + tails[:, 128 * v : 128 * v + 128]).astype(BF16)
    a_buf[mine_z] = a_src[2:3]

    def prepare():
        fc_w[...] = jnp.zeros_like(fc_w)
        gate_w[...] = jnp.zeros_like(gate_w)
        up_w[...] = jnp.zeros_like(up_w)
        down_w[...] = jnp.zeros_like(down_w)
        for load in loads[4:]:
            load.wait()
        fc_w[0:DB, 0:DB] = fc_v[...]
        gate_w[0:DB, 0:FB] = gate_v[...]
        up_w[0:DB, 0:FB] = up_v[...]
        down_w[0:DB, 0:FB] = down_v[...]

    gain = gain_v[...].reshape(1, DB)
    gain = jnp.concatenate([gain, jnp.ones((1, DP - DB), F32)], axis=1)
    packed_row = iota((16, 128), 0)
    gain_p = jnp.where(
        packed_row < 4,
        gain[:, 0:128],
        jnp.where(packed_row < 8, gain[:, 128:256], gain[:, 256:384]),
    )
    pl.semaphore_wait(barrier, len(Z_PEERS) + NF - 1)
    gather_start(0, a_buf, a_src.at[0], a_src.at[1])
    prepare()
    gather_relay(0, a_buf)
    gather_end(0, a_buf)

    slots = a_buf[...].reshape(NZ * CAP, DP)
    before = jnp.where(iota((256, 256), 1) // CAP < iota((256, 256), 0) // CAP, 1.0, 0.0).astype(BF16)
    start = dot(before, slots[:, 256:384])[:, 127:128] * (1.0 / CAP)
    count = slots[:, 256:384].astype(F32)[:, 127:128]
    place = (iota((256, ROWS), 0) % CAP).astype(F32)
    goes = iota((256, ROWS), 1).astype(F32) == start + place
    select = jnp.where((place < count) & goes, 1.0, 0.0).astype(BF16)
    group = seat((z - lax.div(iota((256, 1), 0), CAP) + NZ) % NZ, side) % 128
    lane = iota((256, 128), 1)
    meant = (lane >= group) & (lane < group + PIECE) | (lane < 64)
    tail = jnp.where(meant, slots[:, 256:384].astype(F32), 0.0).astype(BF16)
    slots = jnp.concatenate([slots[:, 0:256], tail], axis=1)
    live = dot(select, slots, 0, 0).astype(BF16)
    fc_part = dot(live, fc_w[...])
    none = jnp.zeros((ROWS, 128), F32)
    pack_into(b1_src, (fc_part[:, 0:128], fc_part[:, 128:256], fc_part[:, 256:384], none))
    b1_dst[mine_f] = b1_src[mine_f]
    send_f(1, b1_src, b1_dst)
    col = iota((128, DP), 1)
    row = iota((128, DP), 0) - 64
    inside = (row >= 0) & (row < 6 * PIECE)
    row = row - ((jnp.where(inside, row, 0) * 205) >> 11) * PIECE
    lay = jnp.where(inside & (col == PIECE * f + row), 1.0, 0.0).astype(BF16)
    target_part = dot(live[:, 256:384], lay)
    wait_f(1, b1_dst)

    def total_f(buf):
        return jnp.sum(buf[...].astype(F32), axis=0)

    mixed = total_f(b1_dst)
    b2_buf[mine_f] = (mixed * gain_p).astype(BF16).reshape(1, 16, 128)
    send_f(2, None, b2_buf)
    wait_f(2, b2_buf)

    h_tiles = unpack(b2_buf[...].astype(F32))
    h = jnp.concatenate(h_tiles[:3], axis=1)
    plain = h / gain
    squares = jnp.sum(plain * plain, axis=1, keepdims=True)
    h = h.astype(BF16)
    gate_part = dot(h, gate_w[...])
    up_part = dot(h, up_w[...])
    sq_high, sq_low = split(squares)
    lane = iota((ROWS, FP), 1)
    gate_part = jnp.where(lane == META, sq_high, jnp.where(lane == META + 1, sq_low, gate_part))
    d1a_src[...] = twin(gate_part[:, CUT:], up_part[:, CUT:]).astype(BF16)
    reduce_start(3, d1a_src, d1a_dst)
    d1b_src[...] = twin(gate_part[:, :CUT], up_part[:, :CUT]).astype(BF16)
    reduce_start(4, d1b_src, d1b_dst)
    reduce_near(3, d1a_src, d1a_dst)
    reduce_near(4, d1b_src, d1b_dst)
    reduce_relay(3, d1a_src, d1a_dst, d1a_mid)
    reduce_relay(4, d1b_src, d1b_dst, d1b_mid)

    both_a = reduce_end(3, d1a_src, d1a_dst)
    lane_a = iota((8, FP - CUT), 1) + CUT
    real = lane_a < FB
    spare = (lane_a == META) | (lane_a == META + 1)
    square = jnp.sum(jnp.where(spare, both_a[0:8], 0.0), axis=1, keepdims=True)
    inverse = lax.rsqrt(square / D + EPS)
    gate_a = jnp.where(real, both_a[0:8] * inverse, 0.0)
    up_a = both_a[8:16] * inverse
    sig_a = jax.nn.sigmoid(gate_a)
    d2a_buf[mine_z] = fold(gate_a * sig_a * up_a).astype(BF16)
    gather_start(5, d2a_buf)

    both_b = reduce_end(4, d1b_src, d1b_dst)
    gate_b = both_b[0:8] * inverse
    up_b = both_b[8:16] * inverse
    sig_b = jax.nn.sigmoid(gate_b)
    d2b_buf[mine_z] = fold(gate_b * sig_b * up_b).astype(BF16)
    gather_start(6, d2b_buf)
    gather_relay(5, d2a_buf)
    gather_relay(6, d2b_buf)

    gather_end(5, d2a_buf)
    act_a = unfold(d2a_buf[...].astype(F32), FP - CUT).astype(BF16)
    down_part = dot(act_a, down_w[:, CUT:], 1, 1) - target_part
    gather_end(6, d2b_buf)
    act_b = unfold(d2b_buf[...].astype(F32), CUT).astype(BF16)
    down_part = down_part + dot(act_b, down_w[:, :CUT], 1, 1)
    pack_into(e1_src, (down_part[:, 0:128], down_part[:, 128:256], down_part[:, 256:384], none))
    e1_dst[mine_f] = e1_src[mine_f]
    send_f(7, e1_src, e1_dst)
    wait_f(7, e1_dst)

    loss_grad = (mixed + total_f(e1_dst)) * SCALE
    e2_buf[mine_f] = loss_grad.astype(BF16).reshape(1, 16, 128)
    send_f(8, None, e2_buf)
    wait_f(8, e2_buf)

    loss_all = jnp.concatenate(unpack(e2_buf[...].astype(F32))[:3], axis=1).astype(BF16)
    f1b_src[...] = fold(dot(loss_all, down_w[:, :CUT])).astype(BF16)
    reduce_start(9, f1b_src, f1b_dst)
    f1a_src[...] = fold(dot(loss_all, down_w[:, CUT:])).astype(BF16)
    reduce_start(10, f1a_src, f1a_dst)
    reduce_near(9, f1b_src, f1b_dst)
    reduce_near(10, f1a_src, f1a_dst)
    reduce_relay(9, f1b_src, f1b_dst, f1b_mid)
    reduce_relay(10, f1a_src, f1a_dst, f1a_mid)

    def back(back_act, gate_pre, up_pre, sig):
        back_gate = back_act * up_pre * sig * (1.0 + gate_pre * (1.0 - sig))
        back_up = back_act * gate_pre * sig
        return back_gate, back_up, back_gate * gate_pre + back_up * up_pre

    back_b = unfold(reduce_end(9, f1b_src, f1b_dst).reshape(1, 16, 256), CUT)
    bg, bu, terms_b = back(back_b, gate_b, up_b, sig_b)
    f2b_buf[mine_z] = twin(bg * inverse, bu * inverse).astype(BF16)
    gather_start(11, f2b_buf)

    back_a = unfold(reduce_end(10, f1a_src, f1a_dst).reshape(1, 16, 256), FP - CUT)
    bg, bu, terms_a = back(back_a, gate_a, up_a, sig_a)
    inner = jnp.sum(jnp.where(real, terms_a, 0.0), axis=1, keepdims=True)
    inner = inverse * inverse / D * (inner + jnp.sum(terms_b, axis=1, keepdims=True))
    in_high, in_low = split(inner)
    bg = jnp.where(real, bg * inverse, 0.0)
    bg = jnp.where(lane_a == META, in_high, jnp.where(lane_a == META + 1, in_low, bg))
    bu = jnp.where(real, bu * inverse, 0.0)
    f2a_buf[mine_z] = twin(bg, bu).astype(BF16)
    gather_start(12, f2a_buf)
    gather_relay(11, f2b_buf)
    gather_relay(12, f2a_buf)
    grad_down_v[:, 0:CUT] = dot(loss_all, act_b, 0, 0)[0:DB]
    grad_down_v[:, CUT:FB] = dot(loss_all, act_a, 0, 0)[0:DB, 0 : FB - CUT]
    leave(4)

    gather_end(11, f2b_buf)
    back_both = f2b_buf[...].astype(F32)
    bg_b = back_both[:, 0:8].reshape(ROWS, CUT).astype(BF16)
    bu_b = back_both[:, 8:16].reshape(ROWS, CUT).astype(BF16)
    norm_part = dot(bg_b, gate_w[:, :CUT], 1, 1) + dot(bu_b, up_w[:, :CUT], 1, 1)
    gather_end(12, f2a_buf)
    back_both = f2a_buf[...].astype(F32)
    bg_a = back_both[:, 0:8].reshape(ROWS, FP - CUT)
    bu_a = back_both[:, 8:16].reshape(ROWS, FP - CUT).astype(BF16)
    lane = iota((ROWS, 128), 1) + 768
    inner_tile = jnp.where((lane == META) | (lane == META + 1), bg_a[:, 768 - CUT :], 0.0)
    bg_a = bg_a.astype(BF16)
    norm_part = norm_part + dot(bg_a, gate_w[:, CUT:], 1, 1) + dot(bu_a, up_w[:, CUT:], 1, 1)
    pack_into(g1_src, (norm_part[:, 0:128], norm_part[:, 128:256], norm_part[:, 256:384], inner_tile))
    g1_dst[mine_f] = g1_src[mine_f]
    send_f(13, g1_src, g1_dst)
    for grad, back_a, back_b in ((grad_gate_v, bg_a, bg_b), (grad_up_v, bu_a, bu_b)):
        grad[:, 0:CUT] = dot(h, back_b, 0, 0)[0:DB].astype(BF16)
        grad[:, CUT:FB] = dot(h, back_a, 0, 0)[0:DB, 0 : FB - CUT].astype(BF16)
    leave(2)
    leave(3)
    wait_f(13, g1_dst)

    back_norm = total_f(g1_dst)
    inner_col = jnp.sum(jnp.where(packed_row >= 12, back_norm, 0.0), axis=1, keepdims=True)
    inner_col = jnp.broadcast_to(inner_col, (16, 128))
    inner_all = pltpu.roll(inner_col, 4, 0) + pltpu.roll(inner_col, 8, 0) + pltpu.roll(inner_col, 12, 0)
    back_mix = loss_grad + gain_p * back_norm - mixed * inner_all
    terms = back_norm * mixed
    gain_sums = [
        jnp.sum(jnp.where(packed_row // 4 == k, terms, 0.0), axis=0, keepdims=True) for k in range(3)
    ]
    for k in range(3):
        back_mix = jnp.where(packed_row == 12 + k, gain_sums[k], back_mix)
    g2_buf[mine_f] = back_mix.astype(BF16).reshape(1, 16, 128)
    send_f(14, None, g2_buf)
    wait_f(14, g2_buf)

    mix_packed = g2_buf[...].astype(F32)
    mix_all = jnp.concatenate(unpack(mix_packed)[:3], axis=1).astype(BF16)
    grad_fc_v[...] = dot(live, mix_all, 0, 0)[0:DB, 0:DB]
    leave(0)
    gain_total = jnp.sum(mix_packed, axis=0)
    gain_line = jnp.concatenate([gain_total[12 + k : 13 + k] for k in range(3)], axis=1)
    grad_gain_v[...] = gain_line[:, 0:DB].reshape(DB)
    leave(1)

    for phase, buf in (
        (0, a_buf),
        (3, d1a_dst),
        (4, d1b_dst),
        (5, d2a_buf),
        (6, d2b_buf),
        (9, f1b_dst),
        (10, f1a_dst),
        (11, f2b_buf),
        (12, f2a_buf),
    ):
        settle(send_sem.at[phase], buf, NZ - 1)
    for phase, buf in ((1, b1_dst), (2, b2_buf), (7, e1_dst), (8, e2_buf), (13, g1_dst), (14, g2_buf)):
        settle(send_sem.at[phase], buf, NF - 1)
    for result in results:
        result.wait()


def store_kernel(*refs):
    sources, targets, held = refs[0:5], refs[5:10], refs[10:15]
    in_sem, out_sem = refs[15:17]
    order = (4, 2, 3, 0, 1)
    loads = {i: pltpu.make_async_copy(sources[i], held[i], in_sem.at[i]) for i in order}
    stores = {i: pltpu.make_async_copy(held[i], targets[i], out_sem.at[i]) for i in order}
    for i in order:
        loads[i].start()
    for i in order:
        loads[i].wait()
        stores[i].start()
    for i in order:
        stores[i].wait()


def shards(
    hidden_rows,
    embed_rows,
    target_rows,
    counts,
    fc_weight,
    norm_gain,
    gate_weight,
    up_weight,
    down_weight,
):
    vmem = pl.BlockSpec(memory_space=pltpu.VMEM)
    hbm = pl.BlockSpec(memory_space=pl.ANY)
    xy = pltpu.VMEM((NF, 16, 128), BF16)
    shapes = (
        jax.ShapeDtypeStruct((DB, DB), F32),
        jax.ShapeDtypeStruct((DB,), F32),
        jax.ShapeDtypeStruct((DB, FB), BF16),
        jax.ShapeDtypeStruct((DB, FB), BF16),
        jax.ShapeDtypeStruct((DB, FB), F32),
    )
    found = pl.pallas_call(
        kernel,
        out_shape=shapes,
        in_specs=[pl.BlockSpec(memory_space=pltpu.SMEM)] + [hbm] * 8,
        out_specs=[hbm] * 5,
        scratch_shapes=[
            pltpu.VMEM((CAP, 160), BF16),
            pltpu.VMEM((CAP, 160), BF16),
            pltpu.VMEM((CAP, D), BF16),
            pltpu.VMEM((DB,), F32),
            pltpu.VMEM((DB, DB), BF16),
            pltpu.VMEM((DB, FB), BF16),
            pltpu.VMEM((DB, FB), BF16),
            pltpu.VMEM((DB, FB), BF16),
            pltpu.VMEM((DP, DP), BF16),
            pltpu.VMEM((DP, FP), BF16),
            pltpu.VMEM((DP, FP), BF16),
            pltpu.VMEM((DP, FP), BF16),
            pltpu.VMEM((3, CAP, DP), BF16),
            pltpu.VMEM((NZ, CAP, DP), BF16),
            xy,
            xy,
            xy,
            pltpu.VMEM((NZ, 16, FP - CUT), BF16),
            pltpu.VMEM((NZ - 1, 16, FP - CUT), BF16),
            pltpu.VMEM((2, 16, FP - CUT), BF16),
            pltpu.VMEM((NZ, 16, CUT), BF16),
            pltpu.VMEM((NZ - 1, 16, CUT), BF16),
            pltpu.VMEM((2, 16, CUT), BF16),
            pltpu.VMEM((NZ, 16, 256), BF16),
            pltpu.VMEM((NZ, 16, 256), BF16),
            xy,
            xy,
            xy,
            pltpu.VMEM((NZ, 16, 256), BF16),
            pltpu.VMEM((NZ - 1, 16, 256), BF16),
            pltpu.VMEM((2, 16, 256), BF16),
            pltpu.VMEM((NZ, 16, 256), BF16),
            pltpu.VMEM((NZ - 1, 16, 256), BF16),
            pltpu.VMEM((2, 16, 256), BF16),
            pltpu.VMEM((NZ, 16, FP - CUT), BF16),
            pltpu.VMEM((NZ, 16, CUT), BF16),
            xy,
            xy,
            xy,
            pltpu.VMEM((DB, DB), F32),
            pltpu.VMEM((DB,), F32),
            pltpu.VMEM((DB, FB), BF16),
            pltpu.VMEM((DB, FB), BF16),
            pltpu.VMEM((DB, FB), F32),
            pltpu.SemaphoreType.DMA((8,)),
            pltpu.SemaphoreType.DMA((5,)),
            pltpu.SemaphoreType.DMA((15,)),
            pltpu.SemaphoreType.DMA((15, 4)),
        ],
        compiler_params=pltpu.CompilerParams(
            collective_id=0, has_side_effects=True, vmem_limit_bytes=56 << 20
        ),
        name="draft_layer",
    )(
        counts,
        hidden_rows,
        embed_rows,
        target_rows,
        norm_gain,
        fc_weight.reshape(DB, DB),
        gate_weight,
        up_weight,
        down_weight.T,
    )
    grad_fc, grad_gain, grad_gate, grad_up, grad_down = pl.pallas_call(
        store_kernel,
        out_shape=shapes,
        in_specs=[hbm] * 5,
        out_specs=[hbm] * 5,
        scratch_shapes=[pltpu.VMEM(shape.shape, shape.dtype) for shape in shapes]
        + [pltpu.SemaphoreType.DMA((5,)), pltpu.SemaphoreType.DMA((5,))],
        name="store_results",
    )(*found)
    return (
        grad_fc.reshape(2, DB // 2, DB),
        grad_gain,
        grad_gate,
        grad_up,
        grad_down.T,
    )


def solution(mesh):
    placed = (
        P("roll", "fsdp"),
        P("roll", "fsdp"),
        P("roll", None),
        P("roll"),
        P(None, "fsdp", "roll"),
        P("roll"),
        P("roll", "fsdp"),
        P("roll", "fsdp"),
        P("fsdp", "roll"),
    )
    return jax.shard_map(
        shards,
        mesh=mesh,
        in_specs=placed,
        out_specs=(
            P(None, "fsdp", "roll"),
            P("roll"),
            P("roll", "fsdp"),
            P("roll", "fsdp"),
            P("fsdp", "roll"),
        ),
        check_vma=False,
    )
```

```python
import math

import jax
import jax.numpy as jnp
from jax import lax
from jax.experimental import pallas as pl
from jax.experimental.pallas import tpu as pltpu
from jax.sharding import PartitionSpec as P

D = 5120
ROWS = 128
CAP = 16
NZ = 16
NF = 32
DB = 320
DP = 384
FB = 800
FP = 896
PIECE = DB // NF
CUT = 512
META = 832
EPS = 1e-06
F_ORDER = sorted(
    ((x, y, c) for x in range(4) for y in range(4) for c in range(2) if x + y + c),
    key=lambda at: -min(at[0], 4 - at[0]) - min(at[1], 4 - at[1]),
)
SCALE = 1.0 / math.sqrt(ROWS)
F32 = jnp.float32
BF16 = jnp.bfloat16
MESH = pl.DeviceIdType.MESH
Z_PEERS = (4, -4, 3, -3, 2, -2, 1, -1)


def dot(a, b, ca=1, cb=0):
    return lax.dot_general(a, b, (((ca,), (cb,)), ((), ())), preferred_element_type=F32)


def iota(shape, axis):
    return lax.broadcasted_iota(jnp.int32, shape, axis)


def pack_into(ref, tiles):
    low = iota((ROWS, 128), 0) % 8 < 4
    k0, k1, k2, k3 = tiles
    down = [pltpu.roll(t, 4, 0) for t in (k1, k3)]
    up = [pltpu.roll(t, ROWS - 4, 0) for t in (k0, k2)]
    even = [jnp.where(low, k0, down[0]), jnp.where(low, k2, down[1])]
    odd = [jnp.where(low, up[0], k1), jnp.where(low, up[1], k3)]
    halves = [jnp.concatenate([t.reshape(16, 8, 128) for t in pair], axis=1) for pair in (even, odd)]
    ref[...] = jnp.stack(halves, axis=1).reshape(NF, 16, 128).astype(ref.dtype)


def unpack(packed):
    packed = packed.reshape(16, 2, 16, 128)
    low = iota((ROWS, 128), 0) % 8 < 4
    e0 = packed[:, 0, 0:8].reshape(ROWS, 128)
    e1 = packed[:, 0, 8:16].reshape(ROWS, 128)
    o0 = packed[:, 1, 0:8].reshape(ROWS, 128)
    o1 = packed[:, 1, 8:16].reshape(ROWS, 128)
    down = [pltpu.roll(t, 4, 0) for t in (o0, o1)]
    up = [pltpu.roll(t, ROWS - 4, 0) for t in (e0, e1)]
    return (
        jnp.where(low, e0, down[0]),
        jnp.where(low, up[0], o0),
        jnp.where(low, e1, down[1]),
        jnp.where(low, up[1], o1),
    )


def split(x):
    high = x.astype(BF16).astype(F32)
    return high, x - high


def fold(x):
    n = x.shape[0] // 8
    tail = x[:, 256:]
    if tail.shape[1] < 256:
        tail = jnp.concatenate([tail, jnp.zeros((n * 8, 128), x.dtype)], axis=1)
    return jnp.concatenate([x[:, :256].reshape(n, 8, 256), tail.reshape(n, 8, 256)], axis=1)


def unfold(x, width):
    n = x.shape[0]
    head = x[:, 0:8].reshape(n * 8, 256)
    tail = x[:, 8:16, 0 : width - 256].reshape(n * 8, width - 256)
    return jnp.concatenate([head, tail], axis=1)


def twin(x, y):
    n, lanes = x.shape[0] // 8, x.shape[1]
    return jnp.concatenate([x.reshape(n, 8, lanes), y.reshape(n, 8, lanes)], axis=1)


def seat(d, side):
    g = jnp.where(d == 0, 4, jnp.where(d == 1, 0, jnp.where(d == 15, 1, jnp.where(d == 2, 2, 3))))
    direct = 256 + 64 + PIECE * g
    up = 64 + PIECE * (d - 3)
    down = 128 + 64 + PIECE * (13 - d)
    rises = (d >= 3) & (d <= 7) | (d == 8) & (side > 0)
    return jnp.where(rises, up, jnp.where((d >= 8) & (d <= 13), down, direct))


def kernel(
    counts_ref,
    hidden_hbm,
    embed_hbm,
    target_hbm,
    gain_hbm,
    fc_hbm,
    gate_hbm,
    up_hbm,
    down_hbm,
    grad_fc_hbm,
    grad_gain_hbm,
    grad_gate_hbm,
    grad_up_hbm,
    grad_down_hbm,
    hidden_v,
    embed_v,
    target_v,
    gain_v,
    fc_v,
    gate_v,
    up_v,
    down_v,
    fc_w,
    gate_w,
    up_w,
    down_w,
    a_src,
    a_buf,
    b1_src,
    b1_dst,
    b2_buf,
    d1a_src,
    d1a_dst,
    d1a_mid,
    d1b_src,
    d1b_dst,
    d1b_mid,
    d2a_buf,
    d2b_buf,
    e1_src,
    e1_dst,
    e2_buf,
    f1a_src,
    f1a_dst,
    f1a_mid,
    f1b_src,
    f1b_dst,
    f1b_mid,
    f2a_buf,
    f2b_buf,
    g1_src,
    g1_dst,
    g2_buf,
    grad_fc_v,
    grad_gain_v,
    grad_gate_v,
    grad_up_v,
    grad_down_v,
    load_sem,
    out_sem,
    send_sem,
    recv_sem,
):
    z = lax.axis_index("roll")
    f = lax.axis_index("fsdp")
    f_x, f_y, f_c = lax.div(f, 8), lax.rem(lax.div(f, 2), 4), lax.rem(f, 2)

    side = 1 - 2 * lax.rem(z, 2)

    def z_at(offset):
        return lax.rem(z + (offset + NZ), NZ)

    def f_peer(i):
        dx, dy, dc = F_ORDER[i]
        x = lax.rem(f_x + dx, 4)
        y = lax.rem(f_y + dy, 4)
        c = f_c if dc == 0 else 1 - f_c
        return x * 8 + y * 2 + c

    loads = [
        pltpu.make_async_copy(a, b, load_sem.at[i])
        for i, (a, b) in enumerate(
            (
                (hidden_hbm, hidden_v),
                (embed_hbm, embed_v),
                (target_hbm, target_v),
                (gain_hbm, gain_v),
                (fc_hbm, fc_v),
                (gate_hbm, gate_v),
                (up_hbm, up_v),
                (down_hbm, down_v),
            )
        )
    ]
    for load in loads:
        load.start()

    barrier = pltpu.get_barrier_semaphore()

    def greet_f(i, c):
        pl.semaphore_signal(barrier, inc=1, device_id=(z, f_peer(i)), device_id_type=MESH)
        return c

    for d in Z_PEERS:
        pl.semaphore_signal(barrier, inc=1, device_id=(z_at(d), f), device_id_type=MESH)
    for i in range(NF - 1):
        greet_f(i, 0)

    def send_z(src, dst, d, phase, group):
        pltpu.make_async_remote_copy(
            src_ref=src,
            dst_ref=dst,
            send_sem=send_sem.at[phase],
            recv_sem=recv_sem.at[phase, group],
            device_id=(z_at(d), f),
            device_id_type=MESH,
        ).start()

    def settle(sem, buf, n):
        part = buf.at[pl.ds(0, n)]
        pltpu.make_async_copy(part, part, sem).wait()

    def gather_start(phase, buf, plus=None, minus=None):
        own = buf.at[z]
        send_z(own if plus is None else plus, own, 4, phase, 0)
        send_z(own if minus is None else minus, own, -4, phase, 1)
        for d in (2, -2, 1, -1):
            send_z(own, own, d, phase, 2)

    def gather_relay(phase, buf):
        settle(recv_sem.at[phase, 0], buf, 1)
        settle(recv_sem.at[phase, 1], buf, 1)
        came = buf.at[z_at(-4 * side)]
        send_z(came, came, 4 * side, phase, 2)
        low, high = buf.at[z_at(-4)], buf.at[z_at(4)]
        for d in (3, 2, 1, -1):
            send_z(low, low, d, phase, 2)
            send_z(high, high, -d, phase, 2)

    def gather_end(phase, buf):
        settle(recv_sem.at[phase, 2], buf, 13)

    def reduce_start(phase, src, dst):
        for own, d, slot, group in (
            (8, -4 * side, 8, 3),
            (7, 3, 3, 0),
            (-7, -3, 7, 1),
            (6, 2, 2, 0),
            (-6, -2, 6, 1),
            (5, 1, 1, 0),
            (-5, -1, 5, 1),
            (3, -1, 0, 0),
            (-3, 1, 4, 1),
        ):
            send_z(src.at[z_at(own)], dst.at[slot], d, phase, group)

    def reduce_near(phase, src, dst):
        for d, slot in ((2, 11), (-2, 12), (1, 13), (-1, 14)):
            send_z(src.at[z_at(d)], dst.at[slot], d, phase, 2)

    def reduce_relay(phase, src, dst, mid):
        settle(recv_sem.at[phase, 3], dst, 1)
        far = dst[8:9].astype(F32)
        for g, d in ((0, 4), (1, -4)):
            settle(recv_sem.at[phase, g], dst, 4)
            total = jnp.sum(dst[4 * g : 4 * g + 4].astype(F32), axis=0, keepdims=True)
            total = total + src[pl.ds(z_at(d), 1)].astype(F32)
            total = total + jnp.where(side * d < 0, far, 0.0)
            mid[g : g + 1] = total.astype(BF16)
            send_z(mid.at[g], dst.at[9 + g], d, phase, 2)

    def reduce_end(phase, src, dst):
        settle(recv_sem.at[phase, 2], dst, 6)
        return jnp.sum(dst[9:15].astype(F32), axis=0) + src[pl.ds(z, 1)].astype(F32)[0]

    def send_f(phase, src, dst):
        def step(i, c):
            p = f_peer(i)
            pltpu.make_async_remote_copy(
                src_ref=dst.at[f] if src is None else src.at[p],
                dst_ref=dst.at[f],
                send_sem=send_sem.at[phase],
                recv_sem=recv_sem.at[phase, 0],
                device_id=(z, p),
                device_id_type=MESH,
            ).start()
            return c

        for i in range(NF - 1):
            step(i, 0)

    def wait_f(phase, buf):
        settle(recv_sem.at[phase, 0], buf, NF - 1)

    results = [
        pltpu.make_async_copy(a, b, out_sem.at[i])
        for i, (a, b) in enumerate(
            (
                (grad_fc_v, grad_fc_hbm),
                (grad_gain_v, grad_gain_hbm),
                (grad_gate_v, grad_gate_hbm),
                (grad_up_v, grad_up_hbm),
                (grad_down_v, grad_down_hbm),
            )
        )
    ]

    def leave(i):
        results[i].start()

    mine_z = pl.ds(z, 1)
    mine_f = pl.ds(f, 1)

    for load in loads[:4]:
        load.wait()
    col = iota((160, DP), 1)
    row = iota((160, DP), 0)
    base = dot(embed_v[...], (col == row).astype(F32).astype(BF16)) + dot(
        hidden_v[...], (col == row + 160).astype(F32).astype(BF16)
    )
    base = jnp.where(iota((CAP, DP), 1) == DP - 1, counts_ref[0].astype(F32), base)
    wide = jnp.concatenate([target_v[:, 640 * p : 640 * p + 640] for p in range(8)], axis=0)
    col = iota((640, 256), 1)
    row = iota((640, 256), 0)
    lane = col % 128
    wanted = row == col // 128 * DB + PIECE * f + lane
    pieces = dot(wide, jnp.where((lane < PIECE) & wanted, 1.0, 0.0).astype(BF16))
    line = [jnp.zeros((CAP, 128), F32), jnp.zeros((CAP, 128), F32)]
    for p in range(NZ):
        piece = pieces[p // 2 * 16 : p // 2 * 16 + 16, p % 2 * 128 : p % 2 * 128 + 128]
        shift = PIECE * p if p < 12 else PIECE * (p - 12)
        line[p // 12] += pltpu.roll(piece, shift, 1) if shift else piece
    line = jnp.concatenate(line, axis=1).astype(BF16)
    r = iota((256, 1), 0)
    r = jnp.where(r < 128, r, r - 8)
    receiver = (r * 205) >> 11
    goal = seat((receiver - z + NZ) % NZ, side) + r - receiver * PIECE
    goal = jnp.where(receiver < NZ, goal, -1)
    spread = jnp.where(goal == iota((256, 3 * 128), 1), 1.0, 0.0).astype(BF16)
    tails = dot(line, spread)
    for v in range(3):
        a_src[v, :, 0:256] = base[:, 0:256].astype(BF16)
        a_src[v, :, 256:384] = (base[:, 256:384] + tails[:, 128 * v : 128 * v + 128]).astype(BF16)
    a_buf[mine_z] = a_src[2:3]

    def prepare():
        fc_w[...] = jnp.zeros_like(fc_w)
        gate_w[...] = jnp.zeros_like(gate_w)
        up_w[...] = jnp.zeros_like(up_w)
        down_w[...] = jnp.zeros_like(down_w)
        for load in loads[4:]:
            load.wait()
        fc_w[0:DB, 0:DB] = fc_v[...]
        gate_w[0:DB, 0:FB] = gate_v[...]
        up_w[0:DB, 0:FB] = up_v[...]
        down_w[0:DB, 0:FB] = down_v[...]

    gain = gain_v[...].reshape(1, DB)
    gain = jnp.concatenate([gain, jnp.ones((1, DP - DB), F32)], axis=1)
    packed_row = iota((16, 128), 0)
    gain_p = jnp.where(
        packed_row < 4,
        gain[:, 0:128],
        jnp.where(packed_row < 8, gain[:, 128:256], gain[:, 256:384]),
    )
    pl.semaphore_wait(barrier, len(Z_PEERS) + NF - 1)
    gather_start(0, a_buf, a_src.at[0], a_src.at[1])
    prepare()
    gather_relay(0, a_buf)
    gather_end(0, a_buf)

    slots = a_buf[...].reshape(NZ * CAP, DP)
    before = jnp.where(iota((256, 256), 1) // CAP < iota((256, 256), 0) // CAP, 1.0, 0.0).astype(BF16)
    start = dot(before, slots[:, 256:384])[:, 127:128] * (1.0 / CAP)
    count = slots[:, 256:384].astype(F32)[:, 127:128]
    place = (iota((256, ROWS), 0) % CAP).astype(F32)
    goes = iota((256, ROWS), 1).astype(F32) == start + place
    select = jnp.where((place < count) & goes, 1.0, 0.0).astype(BF16)
    group = seat((z - lax.div(iota((256, 1), 0), CAP) + NZ) % NZ, side) % 128
    lane = iota((256, 128), 1)
    meant = (lane >= group) & (lane < group + PIECE) | (lane < 64)
    tail = jnp.where(meant, slots[:, 256:384].astype(F32), 0.0).astype(BF16)
    slots = jnp.concatenate([slots[:, 0:256], tail], axis=1)
    live = dot(select, slots, 0, 0).astype(BF16)
    fc_part = dot(live, fc_w[...])
    none = jnp.zeros((ROWS, 128), F32)
    pack_into(b1_src, (fc_part[:, 0:128], fc_part[:, 128:256], fc_part[:, 256:384], none))
    send_f(1, b1_src, b1_dst)
    b1_dst[mine_f] = b1_src[mine_f]
    col = iota((128, DP), 1)
    row = iota((128, DP), 0) - 64
    inside = (row >= 0) & (row < 6 * PIECE)
    row = row - ((jnp.where(inside, row, 0) * 205) >> 11) * PIECE
    lay = jnp.where(inside & (col == PIECE * f + row), 1.0, 0.0).astype(BF16)
    target_part = dot(live[:, 256:384], lay)
    wait_f(1, b1_dst)

    def total_f(buf):
        return jnp.sum(buf[...].astype(F32), axis=0)

    mixed = total_f(b1_dst)
    b2_buf[mine_f] = (mixed * gain_p).astype(BF16).reshape(1, 16, 128)
    send_f(2, None, b2_buf)
    wait_f(2, b2_buf)

    h_tiles = unpack(b2_buf[...].astype(F32))
    h = jnp.concatenate(h_tiles[:3], axis=1)
    plain = h / gain
    squares = jnp.sum(plain * plain, axis=1, keepdims=True)
    h = h.astype(BF16)
    sq_high, sq_low = split(squares)
    lane = iota((ROWS, FP - CUT), 1) + CUT
    gate_part = dot(h, gate_w[:, CUT:])
    gate_part = jnp.where(lane == META, sq_high, jnp.where(lane == META + 1, sq_low, gate_part))
    d1a_src[...] = twin(gate_part, dot(h, up_w[:, CUT:])).astype(BF16)
    reduce_start(3, d1a_src, d1a_dst)
    d1b_src[...] = twin(dot(h, gate_w[:, :CUT]), dot(h, up_w[:, :CUT])).astype(BF16)
    reduce_start(4, d1b_src, d1b_dst)
    reduce_near(3, d1a_src, d1a_dst)
    reduce_near(4, d1b_src, d1b_dst)
    reduce_relay(3, d1a_src, d1a_dst, d1a_mid)
    reduce_relay(4, d1b_src, d1b_dst, d1b_mid)

    both_a = reduce_end(3, d1a_src, d1a_dst)
    lane_a = iota((8, FP - CUT), 1) + CUT
    real = lane_a < FB
    spare = (lane_a == META) | (lane_a == META + 1)
    square = jnp.sum(jnp.where(spare, both_a[0:8], 0.0), axis=1, keepdims=True)
    inverse = lax.rsqrt(square / D + EPS)
    gate_a = jnp.where(real, both_a[0:8] * inverse, 0.0)
    up_a = both_a[8:16] * inverse
    sig_a = jax.nn.sigmoid(gate_a)
    d2a_buf[mine_z] = fold(gate_a * sig_a * up_a).astype(BF16)
    gather_start(5, d2a_buf)

    both_b = reduce_end(4, d1b_src, d1b_dst)
    gate_b = both_b[0:8] * inverse
    up_b = both_b[8:16] * inverse
    sig_b = jax.nn.sigmoid(gate_b)
    d2b_buf[mine_z] = fold(gate_b * sig_b * up_b).astype(BF16)
    gather_start(6, d2b_buf)
    gather_relay(5, d2a_buf)
    gather_relay(6, d2b_buf)

    gather_end(5, d2a_buf)
    act_a = unfold(d2a_buf[...].astype(F32), FP - CUT).astype(BF16)
    down_part = dot(act_a, down_w[:, CUT:], 1, 1) - target_part
    gather_end(6, d2b_buf)
    act_b = unfold(d2b_buf[...].astype(F32), CUT).astype(BF16)
    down_part = down_part + dot(act_b, down_w[:, :CUT], 1, 1)
    pack_into(e1_src, (down_part[:, 0:128], down_part[:, 128:256], down_part[:, 256:384], none))
    send_f(7, e1_src, e1_dst)
    e1_dst[mine_f] = e1_src[mine_f]
    wait_f(7, e1_dst)

    loss_grad = (mixed + total_f(e1_dst)) * SCALE
    e2_buf[mine_f] = loss_grad.astype(BF16).reshape(1, 16, 128)
    send_f(8, None, e2_buf)
    wait_f(8, e2_buf)

    loss_all = jnp.concatenate(unpack(e2_buf[...].astype(F32))[:3], axis=1).astype(BF16)
    f1b_src[...] = fold(dot(loss_all, down_w[:, :CUT])).astype(BF16)
    reduce_start(9, f1b_src, f1b_dst)
    f1a_src[...] = fold(dot(loss_all, down_w[:, CUT:])).astype(BF16)
    reduce_start(10, f1a_src, f1a_dst)
    reduce_near(9, f1b_src, f1b_dst)
    reduce_near(10, f1a_src, f1a_dst)
    reduce_relay(9, f1b_src, f1b_dst, f1b_mid)
    reduce_relay(10, f1a_src, f1a_dst, f1a_mid)

    def back(back_act, gate_pre, up_pre, sig):
        back_gate = back_act * up_pre * sig * (1.0 + gate_pre * (1.0 - sig))
        back_up = back_act * gate_pre * sig
        return back_gate, back_up, back_gate * gate_pre + back_up * up_pre

    back_b = unfold(reduce_end(9, f1b_src, f1b_dst).reshape(1, 16, 256), CUT)
    bg, bu, terms_b = back(back_b, gate_b, up_b, sig_b)
    f2b_buf[mine_z] = twin(bg * inverse, bu * inverse).astype(BF16)
    gather_start(11, f2b_buf)

    back_a = unfold(reduce_end(10, f1a_src, f1a_dst).reshape(1, 16, 256), FP - CUT)
    bg, bu, terms_a = back(back_a, gate_a, up_a, sig_a)
    inner = jnp.sum(jnp.where(real, terms_a, 0.0), axis=1, keepdims=True)
    inner = inverse * inverse / D * (inner + jnp.sum(terms_b, axis=1, keepdims=True))
    in_high, in_low = split(inner)
    bg = jnp.where(real, bg * inverse, 0.0)
    bg = jnp.where(lane_a == META, in_high, jnp.where(lane_a == META + 1, in_low, bg))
    bu = jnp.where(real, bu * inverse, 0.0)
    f2a_buf[mine_z] = twin(bg, bu).astype(BF16)
    gather_start(12, f2a_buf)
    gather_relay(11, f2b_buf)
    gather_relay(12, f2a_buf)
    grad_down_v[:, 0:CUT] = dot(loss_all, act_b, 0, 0)[0:DB]
    grad_down_v[:, CUT:FB] = dot(loss_all, act_a, 0, 0)[0:DB, 0 : FB - CUT]
    leave(4)

    gather_end(11, f2b_buf)
    back_both = f2b_buf[...].astype(F32)
    bg_b = back_both[:, 0:8].reshape(ROWS, CUT).astype(BF16)
    bu_b = back_both[:, 8:16].reshape(ROWS, CUT).astype(BF16)
    norm_part = dot(bg_b, gate_w[:, :CUT], 1, 1) + dot(bu_b, up_w[:, :CUT], 1, 1)
    gather_end(12, f2a_buf)
    back_both = f2a_buf[...].astype(F32)
    bg_a = back_both[:, 0:8].reshape(ROWS, FP - CUT)
    bu_a = back_both[:, 8:16].reshape(ROWS, FP - CUT).astype(BF16)
    lane = iota((ROWS, 128), 1) + 768
    inner_tile = jnp.where((lane == META) | (lane == META + 1), bg_a[:, 768 - CUT :], 0.0)
    bg_a = bg_a.astype(BF16)
    norm_part = norm_part + dot(bg_a, gate_w[:, CUT:], 1, 1) + dot(bu_a, up_w[:, CUT:], 1, 1)
    pack_into(g1_src, (norm_part[:, 0:128], norm_part[:, 128:256], norm_part[:, 256:384], inner_tile))
    send_f(13, g1_src, g1_dst)
    g1_dst[mine_f] = g1_src[mine_f]
    for grad, back_a, back_b in ((grad_gate_v, bg_a, bg_b), (grad_up_v, bu_a, bu_b)):
        grad[:, 0:CUT] = dot(h, back_b, 0, 0)[0:DB].astype(BF16)
        grad[:, CUT:FB] = dot(h, back_a, 0, 0)[0:DB, 0 : FB - CUT].astype(BF16)
    leave(2)
    leave(3)
    wait_f(13, g1_dst)

    back_norm = total_f(g1_dst)
    inner_col = jnp.sum(jnp.where(packed_row >= 12, back_norm, 0.0), axis=1, keepdims=True)
    inner_col = jnp.broadcast_to(inner_col, (16, 128))
    inner_all = pltpu.roll(inner_col, 4, 0) + pltpu.roll(inner_col, 8, 0) + pltpu.roll(inner_col, 12, 0)
    back_mix = loss_grad + gain_p * back_norm - mixed * inner_all
    terms = back_norm * mixed
    gain_sums = [
        jnp.sum(jnp.where(packed_row // 4 == k, terms, 0.0), axis=0, keepdims=True) for k in range(3)
    ]
    for k in range(3):
        back_mix = jnp.where(packed_row == 12 + k, gain_sums[k], back_mix)
    g2_buf[mine_f] = back_mix.astype(BF16).reshape(1, 16, 128)
    send_f(14, None, g2_buf)
    wait_f(14, g2_buf)

    mix_packed = g2_buf[...].astype(F32)
    mix_all = jnp.concatenate(unpack(mix_packed)[:3], axis=1).astype(BF16)
    grad_fc_v[...] = dot(live, mix_all, 0, 0)[0:DB, 0:DB]
    leave(0)
    gain_total = jnp.sum(mix_packed, axis=0)
    gain_line = jnp.concatenate([gain_total[12 + k : 13 + k] for k in range(3)], axis=1)
    grad_gain_v[...] = gain_line[:, 0:DB].reshape(DB)
    leave(1)

    for phase, buf in (
        (0, a_buf),
        (3, d1a_dst),
        (4, d1b_dst),
        (5, d2a_buf),
        (6, d2b_buf),
        (9, f1b_dst),
        (10, f1a_dst),
        (11, f2b_buf),
        (12, f2a_buf),
    ):
        settle(send_sem.at[phase], buf, NZ - 1)
    for phase, buf in ((1, b1_dst), (2, b2_buf), (7, e1_dst), (8, e2_buf), (13, g1_dst), (14, g2_buf)):
        settle(send_sem.at[phase], buf, NF - 1)
    for result in results:
        result.wait()


def store_kernel(*refs):
    sources, targets, held = refs[0:5], refs[5:10], refs[10:15]
    in_sem, out_sem = refs[15:17]
    order = (4, 2, 3, 0, 1)
    loads = {i: pltpu.make_async_copy(sources[i], held[i], in_sem.at[i]) for i in order}
    stores = {i: pltpu.make_async_copy(held[i], targets[i], out_sem.at[i]) for i in order}
    for i in order:
        loads[i].start()
    for i in order:
        loads[i].wait()
        stores[i].start()
    for i in order:
        stores[i].wait()


def shards(
    hidden_rows,
    embed_rows,
    target_rows,
    counts,
    fc_weight,
    norm_gain,
    gate_weight,
    up_weight,
    down_weight,
):
    vmem = pl.BlockSpec(memory_space=pltpu.VMEM)
    hbm = pl.BlockSpec(memory_space=pl.ANY)
    xy = pltpu.VMEM((NF, 16, 128), BF16)
    shapes = (
        jax.ShapeDtypeStruct((DB, DB), F32),
        jax.ShapeDtypeStruct((DB,), F32),
        jax.ShapeDtypeStruct((DB, FB), BF16),
        jax.ShapeDtypeStruct((DB, FB), BF16),
        jax.ShapeDtypeStruct((DB, FB), F32),
    )
    found = pl.pallas_call(
        kernel,
        out_shape=shapes,
        in_specs=[pl.BlockSpec(memory_space=pltpu.SMEM)] + [hbm] * 8,
        out_specs=[hbm] * 5,
        scratch_shapes=[
            pltpu.VMEM((CAP, 160), BF16),
            pltpu.VMEM((CAP, 160), BF16),
            pltpu.VMEM((CAP, D), BF16),
            pltpu.VMEM((DB,), F32),
            pltpu.VMEM((DB, DB), BF16),
            pltpu.VMEM((DB, FB), BF16),
            pltpu.VMEM((DB, FB), BF16),
            pltpu.VMEM((DB, FB), BF16),
            pltpu.VMEM((DP, DP), BF16),
            pltpu.VMEM((DP, FP), BF16),
            pltpu.VMEM((DP, FP), BF16),
            pltpu.VMEM((DP, FP), BF16),
            pltpu.VMEM((3, CAP, DP), BF16),
            pltpu.VMEM((NZ, CAP, DP), BF16),
            xy,
            xy,
            xy,
            pltpu.VMEM((NZ, 16, FP - CUT), BF16),
            pltpu.VMEM((NZ - 1, 16, FP - CUT), BF16),
            pltpu.VMEM((2, 16, FP - CUT), BF16),
            pltpu.VMEM((NZ, 16, CUT), BF16),
            pltpu.VMEM((NZ - 1, 16, CUT), BF16),
            pltpu.VMEM((2, 16, CUT), BF16),
            pltpu.VMEM((NZ, 16, 256), BF16),
            pltpu.VMEM((NZ, 16, 256), BF16),
            xy,
            xy,
            xy,
            pltpu.VMEM((NZ, 16, 256), BF16),
            pltpu.VMEM((NZ - 1, 16, 256), BF16),
            pltpu.VMEM((2, 16, 256), BF16),
            pltpu.VMEM((NZ, 16, 256), BF16),
            pltpu.VMEM((NZ - 1, 16, 256), BF16),
            pltpu.VMEM((2, 16, 256), BF16),
            pltpu.VMEM((NZ, 16, FP - CUT), BF16),
            pltpu.VMEM((NZ, 16, CUT), BF16),
            xy,
            xy,
            xy,
            pltpu.VMEM((DB, DB), F32),
            pltpu.VMEM((DB,), F32),
            pltpu.VMEM((DB, FB), BF16),
            pltpu.VMEM((DB, FB), BF16),
            pltpu.VMEM((DB, FB), F32),
            pltpu.SemaphoreType.DMA((8,)),
            pltpu.SemaphoreType.DMA((5,)),
            pltpu.SemaphoreType.DMA((15,)),
            pltpu.SemaphoreType.DMA((15, 4)),
        ],
        compiler_params=pltpu.CompilerParams(
            collective_id=0, has_side_effects=True, vmem_limit_bytes=56 << 20
        ),
        name="draft_layer",
    )(
        counts,
        hidden_rows,
        embed_rows,
        target_rows,
        norm_gain,
        fc_weight.reshape(DB, DB),
        gate_weight,
        up_weight,
        down_weight.T,
    )
    grad_fc, grad_gain, grad_gate, grad_up, grad_down = pl.pallas_call(
        store_kernel,
        out_shape=shapes,
        in_specs=[hbm] * 5,
        out_specs=[hbm] * 5,
        scratch_shapes=[pltpu.VMEM(shape.shape, shape.dtype) for shape in shapes]
        + [pltpu.SemaphoreType.DMA((5,)), pltpu.SemaphoreType.DMA((5,))],
        name="store_results",
    )(*found)
    return (
        grad_fc.reshape(2, DB // 2, DB),
        grad_gain,
        grad_gate,
        grad_up,
        grad_down.T,
    )


def solution(mesh):
    placed = (
        P("roll", "fsdp"),
        P("roll", "fsdp"),
        P("roll", None),
        P("roll"),
        P(None, "fsdp", "roll"),
        P("roll"),
        P("roll", "fsdp"),
        P("roll", "fsdp"),
        P("fsdp", "roll"),
    )
    return jax.shard_map(
        shards,
        mesh=mesh,
        in_specs=placed,
        out_specs=(
            P(None, "fsdp", "roll"),
            P("roll"),
            P("roll", "fsdp"),
            P("roll", "fsdp"),
            P("fsdp", "roll"),
        ),
        check_vma=False,
    )
```
